128 devices in a mesh: row: 4 (over z_hi, core), col: 32 (over x, y, z_lo).
Axes of the slice: x: 4, y: 4, z: 4 (z_hi: 2, z_lo: 2; z = z_hi * 2 + z_lo), core: 2. Of those that a mesh axis runs over, the one named last changes fastest.
Arguments:
- packed_input_rows: bfloat16 [4096, 8192], P('col', 'row'), may hold values from -6 to 6
- frozen_weight: bfloat16 [8192, 28672], P('row', 'col'), may hold values from -0.0625 to 0.0625
- down_adapters: float32 [16, 16, 8192], P(None, None, 'row'), may hold values from -6 to 6
- up_adapters: float32 [16, 16, 28672], P(None, None, 'col'), may hold values from -6 to 6
- trial_learning_rates: float32 [16], replicated, may hold values from 0.03 to 0.3
- row_trial_index: int32 [4096], replicated, may hold values from 0 to 15, never falling along the last dimension, each value on 1 to 512 neighbouring positions
- output_gradient: bfloat16 [4096, 28672], P('row', 'col'), may hold values from -6 to 6
- keeper_slot: int32 [16], replicated, may hold values from 0 to 15, as said below
Outputs:
- projected: bfloat16 [4096, 28672], P('row', 'col')
- new_down: float32 [16, 16, 8192], P(None, None, 'row')
- new_up: float32 [16, 16, 28672], P(None, None, 'col')
The draws below stay inside these ranges and needn't reach their ends.
Inputs may be any that keep to these rules, and one draw needn't show every extreme that they name: `row_trial_index`: never falls along the rows; every trial owns 1 to 512 rows, one trial exactly 512. `keeper_slot`: exactly 8 slots hold their own index, slot 0 and slot 15 among them; each other slot holds the index of a different one of those.
All inputs are finite; a program needn't handle non-finite values.
Results may differ from the reference program's by a relative error of at most 0.0054.
Values may be sent and summed in bfloat16 or wider, within the bound.
A program may use at most 192 MiB of HBM per device.

```python
import math
import jax
import jax.numpy as jnp
import numpy as np
from jax import lax

D = 8192
F = 28672
ADAPTER_RANK = 16
TRIALS = 16
ROWS = 4096
SEG_MOST = 512


def draw_keeper_slot(key, part):
    key = jax.random.fold_in(key, 7)
    first_key = jax.random.fold_in(key, 1)
    second_key = jax.random.fold_in(key, 2)
    halfway = TRIALS // 2
    middle = (1 + jax.random.permutation(first_key, TRIALS - 2)).astype(jnp.int32)
    ends = jnp.array([0, TRIALS - 1], jnp.int32)
    keepers = jnp.concatenate([ends, middle[:halfway - 2]])
    released = middle[halfway - 2:]
    paired = keepers[jax.random.permutation(second_key, halfway)]
    slots = jnp.zeros((TRIALS,), jnp.int32)
    slots = slots.at[keepers].set(keepers)
    slots = slots.at[released].set(paired)
    return slots


def raised(values, own_key, source, target, blocks, factor):
    def block_of(dim):
        return (jnp.arange(values.shape[dim]) // (values.shape[dim] // blocks)).reshape((-1,) + (1,) * (values.ndim - 1 - dim))

    first = jax.random.permutation(own_key, blocks)[block_of(target)]
    far = (block_of(target) + blocks // 2) % blocks
    return jnp.where((block_of(source) == first) | (block_of(source) == far), factor * values, values)


def block_levels(own_key, shape, shards, least, top_value):
    def one(dim, parts):
        steps = jax.random.uniform(jax.random.fold_in(jax.random.fold_in(own_key, 6), dim), (parts,), jnp.float32, least / len(shards), top_value / len(shards))
        return jnp.repeat(jnp.exp(steps), shape[dim] // parts).reshape((-1,) + (1,) * (len(shape) - dim - 1))

    gain = one(*shards[0])
    for cut in shards[1:]:
        gain = gain * one(*cut)
    return gain


def profile(count, total, limit, skew):
    weights = [(1 << 20) // math.isqrt(grade ** skew) + 1 for grade in range(2, count + 1)]
    rest, given = total - limit - (count - 1), [1] * (count - 1)
    while rest > 0:
        candidates = [i for i in range(count - 1) if given[i] < limit]
        mass, budget = sum([weights[i] for i in candidates]), rest
        for i in candidates:
            extra = min(limit - given[i], max(1, budget * weights[i] // mass), rest)
            given[i] = given[i] + extra
            rest = rest - extra
    return np.array([limit] + given)


def ragged(key, number_of, total, reach, skew):
    if number_of == 2:
        one = jax.random.randint(key, (), max(1, total - reach), min(reach, total - 1) + 1)
        return jnp.stack([one, total - one])
    lengths = jnp.asarray(profile(number_of, total, reach, skew), jnp.int32)
    couples = (number_of - 1) // 2
    donor, taker = lengths[1:1 + 2 * couples:2], lengths[2:2 + 2 * couples:2]
    margin = jnp.minimum(donor - 1, reach - taker)
    moved = jax.random.randint(jax.random.fold_in(key, 1), (couples,), 0, 1 << 20) % (margin + 1)
    lengths = lengths.at[1:1 + 2 * couples:2].set(donor - moved).at[2:2 + 2 * couples:2].set(taker + moved)
    return lengths[jax.random.permutation(jax.random.fold_in(key, 2), number_of)]


def scatter_about(stream_key, extent, deviation, limit, cuts=(), held_as=jnp.bfloat16):
    factor_of = block_levels(stream_key, extent, cuts, -0.22, 0.18) if cuts else 1.0
    values = jax.random.normal(stream_key, extent, jnp.float32) * deviation * factor_of
    return jnp.minimum(jnp.maximum(values, -limit), limit).astype(held_as)


def bell_draw_with(key, extent, deviation, reach, cuts, heavy, held_as=jnp.bfloat16):
    values = deviation * jax.random.normal(key, extent, jnp.float32)
    if cuts:
        values = values * block_levels(key, extent, cuts, -0.22, 0.18)
    return jnp.clip(raised(values, jax.random.fold_in(key, 3), *heavy), -reach, reach).astype(held_as)


def setup_inputs(seed: int = 0) -> dict:
    seeds = jax.random.split(jax.random.key(seed), 9)
    packed_input_rows = scatter_about(seeds[0], (ROWS, D), 1.0, 6.0, ((0, 32), (1, 4)))
    frozen_weight = scatter_about(seeds[1], (D, F), D ** -0.5, 0.0625, ((0, 4), (1, 32)))
    down_adapters = scatter_about(seeds[2], (TRIALS, ADAPTER_RANK, D), 1.0, 6.0, ((2, 4),), jnp.float32)
    up_adapters = scatter_about(seeds[3], (TRIALS, ADAPTER_RANK, F), 1.0, 6.0, ((2, 32),), jnp.float32)
    trial_learning_rates = jnp.clip(jnp.exp(jax.random.uniform(seeds[4], (TRIALS,), jnp.float32, math.log(0.03), math.log(0.3))), 0.03, 0.3)
    row_trial_index = jnp.searchsorted(jnp.cumsum(ragged(seeds[5], TRIALS, ROWS, SEG_MOST, 1)), jnp.arange(ROWS), side="right").astype(jnp.int32)
    output_gradient = bell_draw_with(seeds[6], (ROWS, F), 1.0, 6.0, ((0, 4), (1, 32)), (1, 0, 32, 2.75))
    keeper_slot = draw_keeper_slot(jax.random.fold_in(seeds[8], 71), 0)
    return {"packed_input_rows": packed_input_rows, "frozen_weight": frozen_weight, "down_adapters": down_adapters, "up_adapters": up_adapters, "trial_learning_rates": trial_learning_rates, "row_trial_index": row_trial_index, "output_gradient": output_gradient, "keeper_slot": keeper_slot}


def pick_trial_rows(values, trial_member):
    return jnp.sum(values.reshape(values.shape[0], TRIALS, ADAPTER_RANK) * trial_member[:, :, None], axis=1)


def reference(packed_input_rows, frozen_weight, down_adapters, up_adapters, trial_learning_rates, row_trial_index, output_gradient, keeper_slot):
    adapter_scale = 2.0 / ADAPTER_RANK
    inv_width = D ** -0.5
    trial_labels = jnp.arange(TRIALS, dtype=jnp.int32)
    trial_member = (row_trial_index[:, None] == trial_labels[None, :]).astype(jnp.float32)
    down_flat = down_adapters.astype(jnp.bfloat16).reshape(TRIALS * ADAPTER_RANK, D)
    up_flat = up_adapters.astype(jnp.bfloat16).reshape(TRIALS * ADAPTER_RANK, F)
    contract_last = (((1,), (1,)), ((), ()))
    reduce_leading = (((0,), (0,)), ((), ()))
    projected_all = lax.dot_general(packed_input_rows, down_flat, contract_last, preferred_element_type=jnp.float32)
    hidden = pick_trial_rows(projected_all, trial_member) * inv_width
    hidden_low = hidden.astype(jnp.bfloat16)
    hidden_full = (trial_member.astype(jnp.bfloat16)[:, :, None] * hidden_low[:, None, :]).reshape(ROWS, TRIALS * ADAPTER_RANK)
    frozen_term = jnp.dot(packed_input_rows, frozen_weight, preferred_element_type=jnp.float32)
    rank_hidden = jnp.dot(hidden_full, up_flat, preferred_element_type=jnp.float32)
    projected = (frozen_term + adapter_scale * rank_hidden).astype(jnp.bfloat16)
    gradient_full = lax.dot_general(output_gradient, up_flat, contract_last, preferred_element_type=jnp.float32)
    gradient_rows = pick_trial_rows(gradient_full, trial_member) * adapter_scale
    grad_low = gradient_rows.astype(jnp.bfloat16)
    grad_spread = (trial_member.astype(jnp.bfloat16)[:, :, None] * grad_low[:, None, :]).reshape(ROWS, TRIALS * ADAPTER_RANK)
    down_grad = lax.dot_general(grad_spread, packed_input_rows, reduce_leading, preferred_element_type=jnp.float32) * inv_width
    up_gradient = lax.dot_general(hidden_full, output_gradient, reduce_leading, preferred_element_type=jnp.float32) * adapter_scale
    rates = trial_learning_rates[:, None, None]
    moved_down = down_adapters - rates * down_grad.reshape(TRIALS, ADAPTER_RANK, D)
    moved_up = up_adapters - rates * up_gradient.reshape(TRIALS, ADAPTER_RANK, F)
    picked_trial = (keeper_slot[:, None] == trial_labels[None, :]).astype(jnp.float32)
    new_down = jnp.einsum("st,tkd->skd", picked_trial, moved_down, precision=lax.Precision.HIGHEST)
    new_up = jnp.einsum("st,tkf->skf", picked_trial, moved_up, precision=lax.Precision.HIGHEST)
    return projected, new_down, new_up
```

```python
import functools

import jax
import jax.numpy as jnp
from jax import lax
from jax.experimental import pallas as pl
from jax.experimental.pallas import tpu as pltpu
from jax.sharding import PartitionSpec as P

MESH = pl.DeviceIdType.MESH
D = 8192
RANK = 16
TRIALS = 16
FLAT = RANK * TRIALS
SHARD = 128
PIECE = 64
HALF = 32
SCALE = 2.0 / RANK
INV_WIDTH = D ** (-0.5)

STEPS = (
    (("F", 0),),
    (("L", 0, 0),),
    (("L", 1, 0),),
    (("RF", 0), ("RL", 0, 0)),
    (("F", 1),),
    (("L", 0, 1),),
    (("L", 3, 0),),
    (("L", 2, 0),),
    (("RF", 1), ("RL", 0, 1)),
    (("RL", 1, 0), ("RL", 3, 0)),
    (("L", 1, 1),),
    (("L", 3, 1),),
    (("L", 2, 1),),
    (("RL", 1, 1), ("RL", 3, 1)),
    (("RL", 2, 0), ("RL", 2, 1)),
)
ITEMS = tuple(item for step in STEPS for item in step)
Z_GROUP = 3
GROUPS = len(STEPS) + 1


def offsets(kind, first, last, zz):
    return (first, last, zz, 0) if kind == 0 else (last, first, zz, 1)


def landed(axis, item):
    name, zz = item[0], item[-1]
    kind = axis if name in ("F", "RF") else 1 - axis
    if name == "F":
        return [offsets(kind, 3, 0, zz), offsets(kind, 1, 0, zz)]
    if name == "RF":
        return [offsets(kind, 2, 0, zz)]
    if name == "L":
        return [offsets(kind, item[1], 3, zz), offsets(kind, item[1], 1, zz)]
    return [offsets(kind, item[1], 2, zz)]


def group_pieces():
    groups = []
    for step in STEPS:
        groups.append([piece for axis in (0, 1) for item in step for piece in landed(axis, item)])
    groups.insert(Z_GROUP, [(0, 0, 0, 0), (0, 0, 1, 0), (0, 0, 0, 1), (0, 0, 1, 1)])
    return groups


CODES = [[dx + 4 * dy + 16 * dz + 32 * kind for dx, dy, dz, kind in group] for group in group_pieces()]


def select(index, values):
    out = jnp.int32(values[0])
    for at in range(1, len(values)):
        out = jnp.where(index == at, jnp.int32(values[at]), out)
    return out


def gather_kernel(
    x_ref, w_ref, bounds_ref, grad_ref, hid_ref, up_ref, proj_ref, down_ref,
    xg, w_v, keep, stage, recv_core, total, z_stage, recv_z,
    local_sem, send_sem, recv_sem, z_send, z_recv, core_send, core_recv, far_send, far_recv,
):
    row = lax.axis_index("row")
    col = lax.axis_index("col")
    z_hi, core = row // 2, row % 2
    x, y, z_lo = col // 8, (col // 2) % 4, col % 2

    def base(piece):
        dx, dy, dz, kind = piece
        return ((x + dx) % 4 * 8 + (y + dy) % 4 * 2 + (z_lo + dz) % 2) * SHARD + kind * PIECE

    def neighbour(axis, way):
        if axis == 0:
            return (row, (x + way) % 4 * 8 + y * 2 + z_lo)
        return (row, x * 8 + (y + way) % 4 * 2 + z_lo)

    z_mate = (row, x * 8 + y * 2 + 1 - z_lo)
    core_mate = (z_hi * 2 + 1 - core, col)
    far_mate = ((1 - z_hi) * 2 + core, col)

    own = pltpu.make_async_copy(
        x_ref, xg.at[pl.ds(pl.multiple_of(col * SHARD, SHARD), SHARD)], local_sem.at[0]
    )
    own.start()
    weight = pltpu.make_async_copy(w_ref, w_v, local_sem.at[1])
    weight.start()

    barrier = pltpu.get_barrier_semaphore()
    mates = [neighbour(0, 1), neighbour(0, 3), neighbour(1, 1), neighbour(1, 3), z_mate, core_mate, far_mate]
    for mate in mates:
        pl.semaphore_signal(barrier, inc=1, device_id=mate, device_id_type=MESH)
    pl.semaphore_wait(barrier, len(mates))
    own.wait()

    def remote(start, rows, ssem, rsem, mate):
        spot = xg.at[pl.ds(pl.multiple_of(start, HALF), rows)]
        return pltpu.make_async_remote_copy(
            src_ref=spot, dst_ref=spot, send_sem=ssem, recv_sem=rsem, device_id=mate, device_id_type=MESH
        )

    def sending(axis, way, item):
        name, zz = item[0], item[-1]
        kind = axis if name in ("F", "RF") else 1 - axis
        back = 3 if way == 0 else 1
        if name == "F":
            start, rows = base(offsets(kind, 0, 0, zz)), PIECE
        elif name == "RF":
            start, rows = base(offsets(kind, back, 0, zz)) + way * HALF, HALF
        elif name == "L":
            start, rows = base(offsets(kind, item[1], 0, zz)), PIECE
        else:
            start, rows = base(offsets(kind, item[1], back, zz)) + way * HALF, HALF
        at = ITEMS.index(item)
        return remote(
            start, rows, send_sem.at[axis, way, at], recv_sem.at[axis, way, at],
            neighbour(axis, 1 if way == 0 else 3),
        )

    def receiving(axis, way, item):
        pieces = landed(axis, item)
        if len(pieces) == 2:
            start, rows = base(pieces[way]), PIECE
        else:
            start, rows = base(pieces[0]) + way * HALF, HALF
        at = ITEMS.index(item)
        return remote(
            start, rows, send_sem.at[axis, way, at], recv_sem.at[axis, way, at],
            neighbour(axis, 1 if way == 0 else 3),
        )

    def every(step, action):
        for item in STEPS[step]:
            for axis in (0, 1):
                for way in (0, 1):
                    action(axis, way, item)

    def send(step):
        every(step, lambda *what: sending(*what).start())

    def arrive(step):
        every(step, lambda *what: receiving(*what).wait_recv())

    def z_copy(kind, dz):
        return remote(base((0, 0, dz, kind)), PIECE, z_send.at[kind], z_recv.at[kind], z_mate)

    send(0)
    for kind in (0, 1):
        z_copy(kind, 0).start()
    send(1)
    weight.wait()
    down_ref[...] = jnp.zeros_like(down_ref)
    spread = (
        lax.broadcasted_iota(jnp.int32, (RANK, FLAT), 1) % RANK
        == lax.broadcasted_iota(jnp.int32, (RANK, FLAT), 0)
    ).astype(jnp.bfloat16)

    def expand(low, starts, rows):
        values = jnp.dot(low, spread, preferred_element_type=jnp.float32)
        parts = []
        for at, start in enumerate(starts):
            where = start + lax.broadcasted_iota(jnp.int32, (rows, FLAT), 0)
            inside = (where >= bounds_ref[0:1, :]) & (where < bounds_ref[1:2, :])
            parts.append(jnp.where(inside, values[at * rows:(at + 1) * rows], 0.0).astype(jnp.bfloat16))
        return jnp.concatenate(parts, axis=0)

    def decode(code):
        dx, dy, dz, kind = code % 4, code // 4 % 4, code // 16 % 2, code // 32
        return (x + dx) % 4, base((dx, dy, dz, kind))

    def core_copy(group, pair):
        return pltpu.make_async_remote_copy(
            src_ref=stage.at[group, pair], dst_ref=recv_core.at[group, pair],
            send_sem=core_send.at[group, pair], recv_sem=core_recv.at[group, pair],
            device_id=core_mate, device_id_type=MESH,
        )

    def far_copy(number):
        spot = pl.ds(pl.multiple_of(number * PIECE, PIECE), PIECE)
        return pltpu.make_async_remote_copy(
            src_ref=z_stage.at[spot], dst_ref=recv_z.at[spot],
            send_sem=far_send.at[number], recv_sem=far_recv.at[number],
            device_id=far_mate, device_id_type=MESH,
        )

    def group_codes(group):
        return [decode(select(group, [codes[slot] for codes in CODES])) for slot in range(4)]

    def body(group, carry):
        for step in range(len(STEPS)):
            @pl.when(group == (step if step < Z_GROUP else step + 1))
            def _():
                arrive(step)
                if step == Z_GROUP - 1:
                    for kind in (0, 1):
                        z_copy(kind, 1).wait_recv()
                if step + 2 < len(STEPS):
                    send(step + 2)

        @pl.when(group < GROUPS)
        def _():
            places = group_codes(group)
            starts = [pl.multiple_of(start, PIECE) for _, start in places]
            rows = jnp.concatenate([xg[pl.ds(start, PIECE), :] for start in starts], axis=0)
            product = jnp.dot(rows, w_v[...], preferred_element_type=jnp.float32)
            keep[group % 2] = product
            for pair in (0, 1):
                stage[group, pair] = product[pair * 2 * PIECE:(pair + 1) * 2 * PIECE].astype(jnp.bfloat16)

                @pl.when(places[2 * pair][0] % 2 != core)
                def _():
                    core_copy(group, pair).start()

            low = jnp.concatenate([grad_ref[pl.ds(start, PIECE), :] for start in starts], axis=0)
            down_ref[...] += lax.dot_general(
                expand(low, starts, PIECE), rows, (((0,), (0,)), ((), ())), preferred_element_type=jnp.float32
            )

        @pl.when(group > 0)
        def _():
            past = group - 1
            places = group_codes(past)
            for pair in (0, 1):
                @pl.when(places[2 * pair][0] % 2 == core)
                def _():
                    core_copy(past, pair).wait_recv()
                    for half in (0, 1):
                        plane, start = places[2 * pair + half]
                        number = start % (8 * SHARD) // PIECE
                        spot = pl.ds(pl.multiple_of(number * PIECE, PIECE), PIECE)
                        rows = slice(half * PIECE, (half + 1) * PIECE)
                        summed = (
                            keep[past % 2, pl.ds((2 * pair + half) * PIECE, PIECE), :]
                            + recv_core[past, pair, rows, :].astype(jnp.float32)
                        )

                        @pl.when(plane // 2 == z_hi)
                        def _():
                            total[spot, :] = summed

                        @pl.when(plane // 2 != z_hi)
                        def _():
                            z_stage[spot, :] = summed.astype(jnp.bfloat16)
                            far_copy(number).start()

        return carry

    lax.fori_loop(0, GROUPS + 1, body, 0)

    def finish(number, carry):
        far_copy(number).wait_recv()
        start = pl.multiple_of(number * PIECE, PIECE)
        spot = pl.ds(start, PIECE)
        full = expand(hid_ref[spot, :], [row * 8 * SHARD + start], PIECE)
        adapter = jnp.dot(full, up_ref[...], preferred_element_type=jnp.float32)
        proj_ref[spot, :] = (
            total[spot, :] + recv_z[spot, :].astype(jnp.float32) + SCALE * adapter
        ).astype(jnp.bfloat16)
        return carry

    lax.fori_loop(0, 16, finish, 0)

    for step in range(len(STEPS)):
        every(step, lambda *what: sending(*what).wait_send())
    for kind in (0, 1):
        z_copy(kind, 0).wait_send()

    def drain(number, carry):
        far_copy(number).wait_send()
        return carry

    lax.fori_loop(0, 16, drain, 0)

    def drain_core(group, carry):
        places = group_codes(group)
        for pair in (0, 1):
            @pl.when(places[2 * pair][0] % 2 != core)
            def _():
                core_copy(group, pair).wait_send()

        return carry

    lax.fori_loop(0, GROUPS, drain_core, 0)


def per_device(
    packed_input_rows,
    frozen_weight,
    down_adapters,
    up_adapters,
    trial_learning_rates,
    row_trial_index,
    output_gradient,
    keeper_slot,
):
    width_in, width_out = frozen_weight.shape
    all_rows = row_trial_index.shape[0]
    block_rows = output_gradient.shape[0]
    contract_last = (((1,), (1,)), ((), ()))
    reduce_leading = (((0,), (0,)), ((), ()))
    row, col = lax.axis_index("row"), lax.axis_index("col")
    labels = jnp.arange(TRIALS, dtype=jnp.int32)
    down_flat = down_adapters.astype(jnp.bfloat16).reshape(FLAT, width_in)
    up_flat = up_adapters.astype(jnp.bfloat16).reshape(FLAT, width_out)
    ends = jnp.sum((row_trial_index[None, :] <= labels[:, None]).astype(jnp.int32), axis=1)
    starts = jnp.concatenate([jnp.zeros((1,), jnp.int32), ends[:-1]])
    bounds = jnp.repeat(jnp.stack([starts, ends]), RANK, axis=1)

    def member(start, rows):
        ids = lax.dynamic_slice_in_dim(row_trial_index, start, rows)
        return (ids[:, None] == labels[None, :]).astype(jnp.float32)

    def own_trial(full, start):
        rows = full.shape[0]
        return jnp.sum(full.reshape(rows, TRIALS, RANK) * member(start, rows)[:, :, None], axis=1)

    hidden_full = lax.dot_general(
        packed_input_rows, down_flat, contract_last, preferred_element_type=jnp.float32
    )
    hidden = lax.psum(own_trial(hidden_full, col * SHARD), "row") * INV_WIDTH
    hidden_low = lax.all_gather(hidden.astype(jnp.bfloat16), "col", axis=0, tiled=True)
    hidden_low = lax.dynamic_slice_in_dim(hidden_low, row * block_rows, block_rows)
    gradient_full = lax.dot_general(
        output_gradient, up_flat, contract_last, preferred_element_type=jnp.float32
    )
    gradient = lax.psum(own_trial(gradient_full, row * block_rows), "col") * SCALE
    grad_low = lax.all_gather(gradient.astype(jnp.bfloat16), "row", axis=0, tiled=True)
    hidden_wide = (
        member(row * block_rows, block_rows).astype(jnp.bfloat16)[:, :, None] * hidden_low[:, None, :]
    ).reshape(block_rows, FLAT)
    up_gradient = lax.psum(
        lax.dot_general(hidden_wide, output_gradient, reduce_leading, preferred_element_type=jnp.float32), "row"
    ) * SCALE

    vmem = pl.BlockSpec(memory_space=pltpu.VMEM)
    hbm = pl.BlockSpec(memory_space=pl.ANY)
    dma = pltpu.SemaphoreType.DMA
    projected, down_grad = pl.pallas_call(
        gather_kernel,
        name="gather_project",
        out_shape=(
            jax.ShapeDtypeStruct((block_rows, width_out), jnp.bfloat16),
            jax.ShapeDtypeStruct((FLAT, width_in), jnp.float32),
        ),
        in_specs=[hbm, hbm, vmem, vmem, vmem, vmem],
        out_specs=(vmem, vmem),
        scratch_shapes=[
            pltpu.VMEM((all_rows, width_in), jnp.bfloat16),
            pltpu.VMEM((width_in, width_out), jnp.bfloat16),
            pltpu.VMEM((2, 4 * PIECE, width_out), jnp.float32),
            pltpu.VMEM((GROUPS, 2, 2 * PIECE, width_out), jnp.bfloat16),
            pltpu.VMEM((GROUPS, 2, 2 * PIECE, width_out), jnp.bfloat16),
            pltpu.VMEM((block_rows, width_out), jnp.float32),
            pltpu.VMEM((block_rows, width_out), jnp.bfloat16),
            pltpu.VMEM((block_rows, width_out), jnp.bfloat16),
            dma((2,)),
            dma((2, 2, len(ITEMS))),
            dma((2, 2, len(ITEMS))),
            dma((2,)),
            dma((2,)),
            dma((GROUPS, 2)),
            dma((GROUPS, 2)),
            dma((16,)),
            dma((16,)),
        ],
        compiler_params=pltpu.CompilerParams(
            collective_id=0, has_side_effects=True, vmem_limit_bytes=60 << 20
        ),
        cost_estimate=pl.CostEstimate(flops=20 * 10**9, bytes_accessed=30 << 20, transcendentals=0),
    )(packed_input_rows, frozen_weight, bounds, grad_low, hidden_low, up_flat)

    rates = trial_learning_rates[:, None, None]
    moved_down = down_adapters - rates * (down_grad * INV_WIDTH).reshape(down_adapters.shape)
    moved_up = up_adapters - rates * up_gradient.reshape(up_adapters.shape)
    new_down = jnp.take(moved_down, keeper_slot, axis=0, mode="clip")
    new_up = jnp.take(moved_up, keeper_slot, axis=0, mode="clip")
    return (projected, new_down, new_up)


def solution(mesh):
    in_specs = (
        P("col", "row"),
        P("row", "col"),
        P(None, None, "row"),
        P(None, None, "col"),
        P(),
        P(),
        P("row", "col"),
        P(),
    )
    out_specs = (P("row", "col"), P(None, None, "row"), P(None, None, "col"))
    return jax.shard_map(
        per_device, mesh=mesh, in_specs=in_specs, out_specs=out_specs, check_vma=False
    )
```

```python
import jax
import jax.numpy as jnp
from jax import lax
from jax.experimental import pallas as pl
from jax.experimental.pallas import tpu as pltpu
from jax.sharding import PartitionSpec as P

MESH = pl.DeviceIdType.MESH
D = 8192
RANK = 16
TRIALS = 16
FLAT = RANK * TRIALS
SHARD = 128
PIECE = 64
HALF = 32
SCALE = 2.0 / RANK
INV_WIDTH = D ** (-0.5)

STEPS = (
    (("F", 0),),
    (("L", 0, 0),),
    (("L", 1, 0),),
    (("RF", 0), ("RL", 0, 0)),
    (("F", 1),),
    (("L", 0, 1),),
    (("L", 3, 0),),
    (("L", 2, 0),),
    (("RF", 1), ("RL", 0, 1)),
    (("RL", 1, 0), ("RL", 3, 0)),
    (("L", 1, 1),),
    (("L", 3, 1),),
    (("L", 2, 1),),
    (("RL", 1, 1), ("RL", 3, 1)),
    (("RL", 2, 0), ("RL", 2, 1)),
)
ITEMS = tuple(item for step in STEPS for item in step)
Z_GROUP = 3
GROUPS = len(STEPS) + 1


def offsets(kind, first, last, zz):
    return (first, last, zz, 0) if kind == 0 else (last, first, zz, 1)


def landed(axis, item):
    name, zz = item[0], item[-1]
    kind = axis if name in ("F", "RF") else 1 - axis
    if name == "F":
        return [offsets(kind, 3, 0, zz), offsets(kind, 1, 0, zz)]
    if name == "RF":
        return [offsets(kind, 2, 0, zz)]
    if name == "L":
        return [offsets(kind, item[1], 3, zz), offsets(kind, item[1], 1, zz)]
    return [offsets(kind, item[1], 2, zz)]


def group_pieces():
    groups = []
    for step in STEPS:
        groups.append([piece for axis in (0, 1) for item in step for piece in landed(axis, item)])
    groups.insert(Z_GROUP, [(0, 0, 0, 0), (0, 0, 1, 0), (0, 0, 0, 1), (0, 0, 1, 1)])
    return groups


CODES = [[dx + 4 * dy + 16 * dz + 32 * kind for dx, dy, dz, kind in group] for group in group_pieces()]


def pair_slots():
    seen, slots = [0, 0], []
    for group in group_pieces():
        slots.append([])
        for pair in (0, 1):
            odd = group[2 * pair][0] % 2
            slots[-1].append(seen[odd])
            seen[odd] += 1
    return slots


SLOTS = pair_slots()
PAIRS = 16
SMALL = (
    ["hid_core", "hid_far", "hid_z"] + [f"hid_y{k}" for k in (1, 2, 3)] + [f"hid_x{k}" for k in (1, 2, 3)]
    + [f"grad_x{k}" for k in (1, 2, 3)] + [f"grad_y{k}" for k in (1, 2, 3)] + ["grad_z"]
    + [f"low_x{k}" for k in (1, 2, 3)] + ["low_core", "low_far", "up_core", "up_far", "up_share"]
)
CATCH_UP = 6


def select(index, values):
    out = jnp.int32(values[0])
    for at in range(1, len(values)):
        out = jnp.where(index == at, jnp.int32(values[at]), out)
    return out


def whole_kernel(
    x_ref, w_ref, down_ref, up_ref, rate_ref, trial_ref, grad_ref, keeper_ref,
    proj_ref, new_down_ref, new_up_ref,
    xg, w_v, keep, stage, recv_core, total, z_stage, recv_z,
    down_v, down_low, up_v, up_low, grad_v, down_sum, grad_wide, hid_wide,
    hid_part, hid_core, hid_half, hid_far, hid_low,
    grad_part, grad_x, grad_y, grad_z, grad_low,
    up_part, up_core, up_half, up_far, up_sum,
    local_sem, send_sem, recv_sem, z_send, z_recv, core_send, core_recv, far_send, far_recv,
    small_send, small_recv,
):
    row = lax.axis_index("row")
    col = lax.axis_index("col")
    z_hi, core = row // 2, row % 2
    x, y, z_lo = col // 8, (col // 2) % 4, col % 2
    contract_last = (((1,), (1,)), ((), ()))
    contract_first = (((0,), (0,)), ((), ()))

    def base(piece):
        dx, dy, dz, kind = piece
        return ((x + dx) % 4 * 8 + (y + dy) % 4 * 2 + (z_lo + dz) % 2) * SHARD + kind * PIECE

    def neighbour(axis, way):
        if axis == 0:
            return (row, (x + way) % 4 * 8 + y * 2 + z_lo)
        return (row, x * 8 + (y + way) % 4 * 2 + z_lo)

    z_mate = (row, x * 8 + y * 2 + 1 - z_lo)
    core_mate = (z_hi * 2 + 1 - core, col)
    far_mate = ((1 - z_hi) * 2 + core, col)

    loads = [
        pltpu.make_async_copy(source, target, local_sem.at[at])
        for at, (source, target) in enumerate((
            (x_ref, xg.at[pl.ds(pl.multiple_of(col * SHARD, SHARD), SHARD)]),
            (down_ref, down_v), (up_ref, up_v), (grad_ref, grad_v), (w_ref, w_v),
        ))
    ]
    for load in loads:
        load.start()
    own, down_load, up_load, grad_load, weight_load = loads

    barrier = pltpu.get_barrier_semaphore()
    mates = [neighbour(axis, way) for axis in (0, 1) for way in (1, 2, 3)] + [z_mate, core_mate, far_mate]
    for mate in mates:
        pl.semaphore_signal(barrier, inc=1, device_id=mate, device_id_type=MESH)
    pl.semaphore_wait(barrier, len(mates))
    own.wait()

    def remote(start, rows, ssem, rsem, mate):
        spot = xg.at[pl.ds(pl.multiple_of(start, HALF), rows)]
        return pltpu.make_async_remote_copy(
            src_ref=spot, dst_ref=spot, send_sem=ssem, recv_sem=rsem, device_id=mate, device_id_type=MESH
        )

    def sending(axis, way, item):
        name, zz = item[0], item[-1]
        kind = axis if name in ("F", "RF") else 1 - axis
        back = 3 if way == 0 else 1
        if name == "F":
            start, rows = base(offsets(kind, 0, 0, zz)), PIECE
        elif name == "RF":
            start, rows = base(offsets(kind, back, 0, zz)) + way * HALF, HALF
        elif name == "L":
            start, rows = base(offsets(kind, item[1], 0, zz)), PIECE
        else:
            start, rows = base(offsets(kind, item[1], back, zz)) + way * HALF, HALF
        at = ITEMS.index(item)
        return remote(
            start, rows, send_sem.at[axis, way, at], recv_sem.at[axis, way, at],
            neighbour(axis, 1 if way == 0 else 3),
        )

    def receiving(axis, way, item):
        pieces = landed(axis, item)
        if len(pieces) == 2:
            start, rows = base(pieces[way]), PIECE
        else:
            start, rows = base(pieces[0]) + way * HALF, HALF
        at = ITEMS.index(item)
        return remote(
            start, rows, send_sem.at[axis, way, at], recv_sem.at[axis, way, at],
            neighbour(axis, 1 if way == 0 else 3),
        )

    def every(step, action):
        for item in STEPS[step]:
            for axis in (0, 1):
                for way in (0, 1):
                    action(axis, way, item)

    def send(step):
        every(step, lambda *what: sending(*what).start())

    def arrive(step):
        every(step, lambda *what: receiving(*what).wait_recv())

    def z_copy(kind, dz):
        return remote(base((0, 0, dz, kind)), PIECE, z_send.at[kind], z_recv.at[kind], z_mate)

    send(0)
    for kind in (0, 1):
        z_copy(kind, 0).start()
    send(1)

    def small(name, source, target, mate):
        at = SMALL.index(name)
        return pltpu.make_async_remote_copy(
            src_ref=source, dst_ref=target, send_sem=small_send.at[at], recv_sem=small_recv.at[at],
            device_id=mate, device_id_type=MESH,
        )

    half = pl.ds(core * (TRIALS // 2), TRIALS // 2)
    other_half = pl.ds((1 - core) * (TRIALS // 2), TRIALS // 2)
    sends = {
        "hid_core": lambda: small("hid_core", hid_part, hid_core, core_mate),
        "hid_far": lambda: small("hid_far", hid_half, hid_far, far_mate),
        "hid_z": lambda: small("hid_z", hid_low.at[col], hid_low.at[col], z_mate),
        "grad_z": lambda: small("grad_z", grad_z.at[z_lo], grad_z.at[z_lo], z_mate),
        "low_core": lambda: small(
            "low_core", grad_low.at[pl.ds(row * 4, 4)], grad_low.at[pl.ds(row * 4, 4)], core_mate),
        "low_far": lambda: small(
            "low_far", grad_low.at[pl.ds(z_hi * 8, 8)], grad_low.at[pl.ds(z_hi * 8, 8)], far_mate),
        "up_core": lambda: small("up_core", up_part.at[other_half], up_core, core_mate),
        "up_far": lambda: small("up_far", up_half, up_far, far_mate),
        "up_share": lambda: small("up_share", up_sum.at[half], up_sum.at[half], core_mate),
    }
    for way in (1, 2, 3):
        def along(way=way):
            to_x, to_y = neighbour(0, way), neighbour(1, way)
            block, plane = pl.ds(x * 8 + y * 2, 2), pl.ds(x * 8, 8)
            sends[f"hid_y{way}"] = lambda: small(f"hid_y{way}", hid_low.at[block], hid_low.at[block], to_y)
            sends[f"hid_x{way}"] = lambda: small(f"hid_x{way}", hid_low.at[plane], hid_low.at[plane], to_x)
            sends[f"grad_x{way}"] = lambda: small(
                f"grad_x{way}", grad_part.at[(x + way) % 4], grad_x.at[x], to_x)
            sends[f"grad_y{way}"] = lambda: small(f"grad_y{way}", grad_y.at[y], grad_y.at[y], to_y)
            own_chunk = row * 4 + x
            sends[f"low_x{way}"] = lambda: small(
                f"low_x{way}", grad_low.at[own_chunk], grad_low.at[own_chunk], to_x)
        along()

    def go(*names):
        for name in names:
            sends[name]().start()

    def come(*names):
        for name in names:
            sends[name]().wait_recv()

    def trio(name):
        return [f"{name}{way}" for way in (1, 2, 3)]

    def bounds(shape, axis):
        label = lax.broadcasted_iota(jnp.int32, shape, axis) // RANK
        low, high = jnp.zeros(shape, jnp.int32), jnp.zeros(shape, jnp.int32)
        first = jnp.zeros((1, 1), jnp.int32)
        for trial in range(TRIALS):
            count = jnp.sum((trial_ref[...] <= trial).astype(jnp.int32), keepdims=True)
            low = jnp.where(label == trial, first, low)
            high = jnp.where(label == trial, count, high)
            first = count
        return low, high

    lane_low, lane_high = bounds((1, FLAT), 1)
    side_low, side_high = bounds((FLAT, 1), 0)
    spread = (
        lax.broadcasted_iota(jnp.int32, (RANK, FLAT), 1) % RANK
        == lax.broadcasted_iota(jnp.int32, (RANK, FLAT), 0)
    ).astype(jnp.bfloat16)

    def pick_rank(full, start):
        rows = full.shape[1]
        where = start + lax.broadcasted_iota(jnp.int32, (FLAT, rows), 1)
        mine = jnp.where((where >= side_low) & (where < side_high), full, 0.0)
        return jnp.sum(mine.reshape(TRIALS, RANK, rows), axis=0)

    def widen(low, start):
        values = lax.dot_general(low, spread, contract_first, preferred_element_type=jnp.float32)
        where = start + lax.broadcasted_iota(jnp.int32, values.shape, 0)
        return jnp.where((where >= lane_low) & (where < lane_high), values, 0.0).astype(jnp.bfloat16)

    down_load.wait()

    def cast_down(trial, carry):
        down_low[pl.ds(pl.multiple_of(trial * RANK, RANK), RANK), :] = down_v[trial].astype(jnp.bfloat16)
        return carry

    lax.fori_loop(0, TRIALS, cast_down, 0)
    own_rows = xg[pl.ds(pl.multiple_of(col * SHARD, SHARD), SHARD), :]
    hid_part[...] = pick_rank(
        lax.dot_general(down_low[...], own_rows, contract_last, preferred_element_type=jnp.float32), col * SHARD
    )
    go("hid_core")

    up_load.wait()
    for trial in range(TRIALS):
        up_low[trial * RANK:(trial + 1) * RANK, :] = up_v[trial].astype(jnp.bfloat16)
    grad_load.wait()

    def gradient_chunk(chunk, carry):
        start = pl.multiple_of(chunk * 256, 256)
        full = lax.dot_general(
            up_low[...], grad_v[pl.ds(start, 256), :], contract_last, preferred_element_type=jnp.float32
        )
        grad_part[chunk] = pick_rank(full, row * 8 * SHARD + start)
        return carry

    lax.fori_loop(0, 4, gradient_chunk, 0)
    go(*trio("grad_x"))
    grad_x[x] = grad_part[x]
    down_sum[...] = jnp.zeros_like(down_sum)
    total[...] = jnp.zeros_like(total)
    weight_load.wait()

    def small_0():
        come("hid_core")
        hid_half[...] = hid_part[...] + hid_core[...]
        go("hid_far")
        come(*trio("grad_x"))
        grad_y[y] = (grad_x[0] + grad_x[1]) + (grad_x[2] + grad_x[3])
        go(*trio("grad_y"))

    def small_1():
        come("hid_far")
        hid_low[col] = ((hid_half[...] + hid_far[...]) * INV_WIDTH).astype(jnp.bfloat16)
        go("hid_z")
        come(*trio("grad_y"))
        grad_z[z_lo] = (grad_y[0] + grad_y[1]) + (grad_y[2] + grad_y[3])
        go("grad_z")

    def small_2():
        come("hid_z")
        go(*trio("hid_y"))
        come("grad_z")
        grad_low[row * 4 + x] = ((grad_z[0] + grad_z[1]) * SCALE).astype(jnp.bfloat16)
        go(*trio("low_x"))

    def small_3():
        come(*trio("hid_y"))

        @pl.when(x == row)
        def _():
            go(*trio("hid_x"))

        come(*trio("low_x"))
        go("low_core")

    def small_4():
        for way in (1, 2, 3):
            @pl.when((x - way + 4) % 4 == row)
            def _():
                sends[f"hid_x{way}"]().wait_recv()

        def wide(block, carry):
            start = pl.multiple_of(block * SHARD, SHARD)
            hid_wide[pl.ds(start, SHARD), :] = widen(hid_low[row * 8 + block], row * 8 * SHARD + start)
            return carry

        lax.fori_loop(0, 8, wide, 0)
        full = lax.dot_general(hid_wide[...], grad_v[...], contract_first, preferred_element_type=jnp.float32)
        up_part[...] = full.reshape(up_part.shape)
        go("up_core")
        come("low_core")
        go("low_far")

    def small_5():
        come("up_core")
        up_half[...] = up_part[half] + up_core[...]
        go("up_far")
        come("low_far")

        def wide(chunk, carry):
            start = pl.multiple_of(chunk * 256, 256)
            grad_wide[pl.ds(start, 256), :] = widen(grad_low[chunk], start)
            return carry

        lax.fori_loop(0, 16, wide, 0)

    def small_6():
        come("up_far")
        up_sum[half] = up_half[...] + up_far[...]
        go("up_share")

    def small_7():
        come("up_share")

        def moved(slot, carry):
            trial = keeper_ref[slot]
            new_up_ref[slot] = up_v[trial] - rate_ref[trial] * (up_sum[trial] * SCALE)
            return carry

        lax.fori_loop(0, TRIALS, moved, 0)

    def small_8():
        def adapter(block, carry):
            spot = pl.ds(pl.multiple_of(block * SHARD, SHARD), SHARD)
            total[spot, :] += SCALE * jnp.dot(
                hid_wide[spot, :], up_low[...], preferred_element_type=jnp.float32
            )
            return carry

        lax.fori_loop(0, 8, adapter, 0)

    smalls = [small_0, small_1, small_2, small_3, small_4, small_5, small_6, small_7, small_8]

    def decode(code):
        dx, dy, dz, kind = code % 4, code // 4 % 4, code // 16 % 2, code // 32
        return (x + dx) % 4, base((dx, dy, dz, kind))

    def core_copy(slot):
        return pltpu.make_async_remote_copy(
            src_ref=stage.at[slot], dst_ref=recv_core.at[slot],
            send_sem=core_send.at[slot], recv_sem=core_recv.at[slot],
            device_id=core_mate, device_id_type=MESH,
        )

    def far_copy(number):
        spot = pl.ds(pl.multiple_of(number * PIECE, PIECE), PIECE)
        return pltpu.make_async_remote_copy(
            src_ref=z_stage.at[spot], dst_ref=recv_z.at[spot],
            send_sem=far_send.at[number], recv_sem=far_recv.at[number],
            device_id=far_mate, device_id_type=MESH,
        )

    def group_places(group):
        return [decode(select(group, [codes[slot] for codes in CODES])) for slot in range(4)]

    def group_rows(places):
        starts = [pl.multiple_of(start, PIECE) for _, start in places]
        return starts, jnp.concatenate([xg[pl.ds(start, PIECE), :] for start in starts], axis=0)

    def add_down(starts, rows):
        wide = jnp.concatenate([grad_wide[pl.ds(start, PIECE), :] for start in starts], axis=0)
        down_sum[...] += lax.dot_general(
            wide, rows, contract_first, preferred_element_type=jnp.float32
        ).reshape(down_sum.shape)

    def body(group, carry):
        for step in range(len(STEPS)):
            @pl.when(group == (step if step < Z_GROUP else step + 1))
            def _():
                arrive(step)
                if step == Z_GROUP - 1:
                    for kind in (0, 1):
                        z_copy(kind, 1).wait_recv()
                if step + 2 < len(STEPS):
                    send(step + 2)

        @pl.when(group < GROUPS)
        def _():
            places = group_places(group)
            starts, rows = group_rows(places)
            product = jnp.dot(rows, w_v[...], preferred_element_type=jnp.float32)
            keep[group % 2] = product
            for pair in (0, 1):
                @pl.when(places[2 * pair][0] % 2 != core)
                def _():
                    slot = select(group, [slots[pair] for slots in SLOTS])
                    stage[slot] = product[pair * 2 * PIECE:(pair + 1) * 2 * PIECE].astype(jnp.bfloat16)
                    core_copy(slot).start()

        @pl.when(group > 0)
        def _():
            past = group - 1
            places = group_places(past)
            for pair in (0, 1):
                @pl.when(places[2 * pair][0] % 2 == core)
                def _():
                    slot = select(past, [slots[pair] for slots in SLOTS])
                    core_copy(slot).wait_recv()
                    for part in (0, 1):
                        plane, start = places[2 * pair + part]
                        number = start % (8 * SHARD) // PIECE
                        spot = pl.ds(pl.multiple_of(number * PIECE, PIECE), PIECE)
                        summed = (
                            keep[past % 2, pl.ds((2 * pair + part) * PIECE, PIECE), :]
                            + recv_core[slot, part * PIECE:(part + 1) * PIECE, :].astype(jnp.float32)
                        )

                        @pl.when(plane // 2 == z_hi)
                        def _():
                            total[spot, :] += summed

                        @pl.when(plane // 2 != z_hi)
                        def _():
                            z_stage[spot, :] = summed.astype(jnp.bfloat16)
                            far_copy(number).start()

        for at, work in enumerate(smalls):
            pl.when(group == at)(work)

        @pl.when((group >= CATCH_UP) & (group < GROUPS))
        def _():
            add_down(*group_rows(group_places(group)))

        @pl.when((group >= CATCH_UP) & (group < 2 * CATCH_UP))
        def _():
            add_down(*group_rows(group_places(group - CATCH_UP)))

        return carry

    lax.fori_loop(0, GROUPS + 1, body, 0)

    def moved_down(slot, carry):
        trial = keeper_ref[slot]
        new_down_ref[slot] = down_v[trial] - rate_ref[trial] * (down_sum[trial] * INV_WIDTH)
        return carry

    lax.fori_loop(0, TRIALS, moved_down, 0)

    def finish(number, carry):
        far_copy(number).wait_recv()
        spot = pl.ds(pl.multiple_of(number * PIECE, PIECE), PIECE)
        proj_ref[spot, :] = (total[spot, :] + recv_z[spot, :].astype(jnp.float32)).astype(jnp.bfloat16)
        return carry

    lax.fori_loop(0, 16, finish, 0)

    for step in range(len(STEPS)):
        every(step, lambda *what: sending(*what).wait_send())
    for kind in (0, 1):
        z_copy(kind, 0).wait_send()
    for name in SMALL:
        if not name.startswith("hid_x"):
            sends[name]().wait_send()

    @pl.when(x == row)
    def _():
        for name in trio("hid_x"):
            sends[name]().wait_send()

    def drain(number, carry):
        far_copy(number).wait_send()
        core_copy(number).wait_send()
        return carry

    lax.fori_loop(0, 16, drain, 0)


def per_device(
    packed_input_rows,
    frozen_weight,
    down_adapters,
    up_adapters,
    trial_learning_rates,
    row_trial_index,
    output_gradient,
    keeper_slot,
):
    width_in, width_out = frozen_weight.shape
    all_rows = row_trial_index.shape[0]
    block_rows = output_gradient.shape[0]
    vmem = pl.BlockSpec(memory_space=pltpu.VMEM)
    smem = pl.BlockSpec(memory_space=pltpu.SMEM)
    hbm = pl.BlockSpec(memory_space=pl.ANY)
    dma = pltpu.SemaphoreType.DMA
    f32, bf16 = jnp.float32, jnp.bfloat16
    half = TRIALS // 2
    return pl.pallas_call(
        whole_kernel,
        name="adapter_sweep",
        out_shape=(
            jax.ShapeDtypeStruct((block_rows, width_out), bf16),
            jax.ShapeDtypeStruct(down_adapters.shape, f32),
            jax.ShapeDtypeStruct(up_adapters.shape, f32),
        ),
        in_specs=[hbm, hbm, hbm, hbm, smem, vmem, hbm, smem],
        out_specs=(vmem, vmem, vmem),
        scratch_shapes=[
            pltpu.VMEM((all_rows, width_in), bf16),
            pltpu.VMEM((width_in, width_out), bf16),
            pltpu.VMEM((2, 4 * PIECE, width_out), f32),
            pltpu.VMEM((PAIRS, 2 * PIECE, width_out), bf16),
            pltpu.VMEM((PAIRS, 2 * PIECE, width_out), bf16),
            pltpu.VMEM((block_rows, width_out), f32),
            pltpu.VMEM((block_rows, width_out), bf16),
            pltpu.VMEM((block_rows, width_out), bf16),
            pltpu.VMEM(down_adapters.shape, f32),
            pltpu.VMEM((FLAT, width_in), bf16),
            pltpu.VMEM(up_adapters.shape, f32),
            pltpu.VMEM((FLAT, width_out), bf16),
            pltpu.VMEM((block_rows, width_out), bf16),
            pltpu.VMEM(down_adapters.shape, f32),
            pltpu.VMEM((all_rows, FLAT), bf16),
            pltpu.VMEM((block_rows, FLAT), bf16),
            pltpu.VMEM((RANK, SHARD), f32),
            pltpu.VMEM((RANK, SHARD), f32),
            pltpu.VMEM((RANK, SHARD), f32),
            pltpu.VMEM((RANK, SHARD), f32),
            pltpu.VMEM((32, RANK, SHARD), bf16),
            pltpu.VMEM((4, RANK, 256), f32),
            pltpu.VMEM((4, RANK, 256), f32),
            pltpu.VMEM((4, RANK, 256), f32),
            pltpu.VMEM((2, RANK, 256), f32),
            pltpu.VMEM((16, RANK, 256), bf16),
            pltpu.VMEM((TRIALS, RANK, width_out), f32),
            pltpu.VMEM((half, RANK, width_out), f32),
            pltpu.VMEM((half, RANK, width_out), f32),
            pltpu.VMEM((half, RANK, width_out), f32),
            pltpu.VMEM((TRIALS, RANK, width_out), f32),
            dma((5,)),
            dma((2, 2, len(ITEMS))),
            dma((2, 2, len(ITEMS))),
            dma((2,)),
            dma((2,)),
            dma((PAIRS,)),
            dma((PAIRS,)),
            dma((16,)),
            dma((16,)),
            dma((len(SMALL),)),
            dma((len(SMALL),)),
        ],
        compiler_params=pltpu.CompilerParams(
            collective_id=0, has_side_effects=True, vmem_limit_bytes=63 << 20
        ),
        cost_estimate=pl.CostEstimate(flops=22 * 10**9, bytes_accessed=20 << 20, transcendentals=0),
    )(
        packed_input_rows, frozen_weight, down_adapters, up_adapters, trial_learning_rates,
        row_trial_index.reshape(32, all_rows // 32), output_gradient, keeper_slot,
    )


def solution(mesh):
    in_specs = (
        P("col", "row"),
        P("row", "col"),
        P(None, None, "row"),
        P(None, None, "col"),
        P(),
        P(),
        P("row", "col"),
        P(),
    )
    out_specs = (P("row", "col"), P(None, None, "row"), P(None, None, "col"))
    return jax.shard_map(
        per_device, mesh=mesh, in_specs=in_specs, out_specs=out_specs, check_vma=False
    )
```

```python
import jax
import jax.numpy as jnp
from jax import lax
from jax.experimental import pallas as pl
from jax.experimental.pallas import tpu as pltpu
from jax.sharding import PartitionSpec as P

MESH = pl.DeviceIdType.MESH
D = 8192
RANK = 16
TRIALS = 16
FLAT = RANK * TRIALS
SHARD = 128
PIECE = 64
HALF = 32
SCALE = 2.0 / RANK
INV_WIDTH = D ** (-0.5)

STEPS = (
    (("F", 0),),
    (("L", 0, 0),),
    (("L", 1, 0),),
    (("RF", 0), ("RL", 0, 0)),
    (("F", 1),),
    (("L", 0, 1),),
    (("L", 3, 0),),
    (("L", 2, 0),),
    (("RF", 1), ("RL", 0, 1)),
    (("RL", 1, 0), ("RL", 3, 0)),
    (("L", 1, 1),),
    (("L", 3, 1),),
    (("L", 2, 1),),
    (("RL", 1, 1), ("RL", 3, 1)),
    (("RL", 2, 0), ("RL", 2, 1)),
)
ITEMS = tuple(item for step in STEPS for item in step)
Z_GROUP = 3
GROUPS = len(STEPS) + 1


def offsets(kind, first, last, zz):
    return (first, last, zz, 0) if kind == 0 else (last, first, zz, 1)


def landed(axis, item):
    name, zz = item[0], item[-1]
    kind = axis if name in ("F", "RF") else 1 - axis
    if name == "F":
        return [offsets(kind, 3, 0, zz), offsets(kind, 1, 0, zz)]
    if name == "RF":
        return [offsets(kind, 2, 0, zz)]
    if name == "L":
        return [offsets(kind, item[1], 3, zz), offsets(kind, item[1], 1, zz)]
    return [offsets(kind, item[1], 2, zz)]


def group_pieces():
    groups = []
    for step in STEPS:
        groups.append([piece for axis in (0, 1) for item in step for piece in landed(axis, item)])
    groups.insert(Z_GROUP, [(0, 0, 0, 0), (0, 0, 1, 0), (0, 0, 0, 1), (0, 0, 1, 1)])
    return groups


CODES = [[dx + 4 * dy + 16 * dz + 32 * kind for dx, dy, dz, kind in group] for group in group_pieces()]


def pair_slots():
    seen, slots = [0, 0], []
    for group in group_pieces():
        slots.append([])
        for pair in (0, 1):
            odd = group[2 * pair][0] % 2
            slots[-1].append(seen[odd])
            seen[odd] += 1
    return slots


SLOTS = pair_slots()
PAIRS = 16
SMALL = (
    ["hid_core", "hid_far", "hid_z"] + [f"hid_y{k}" for k in (1, 2, 3)] + [f"hid_x{k}" for k in (1, 2, 3)]
    + [f"grad_x{k}" for k in (1, 2, 3)] + [f"grad_y{k}" for k in (1, 2, 3)] + ["grad_z"]
    + [f"low_x{k}" for k in (1, 2, 3)] + ["low_core", "low_far", "up_core", "up_far", "up_share"]
)
FINISH, FINISH_LAG = 9, 3
CATCH_UP = 11


def select(index, values):
    out = jnp.int32(values[0])
    for at in range(1, len(values)):
        out = jnp.where(index == at, jnp.int32(values[at]), out)
    return out


def whole_kernel(
    x_ref, w_ref, down_ref, up_ref, rate_ref, trial_ref, grad_ref, keeper_ref,
    proj_ref, new_down_ref, new_up_ref,
    xg, w_v, keep, stage, recv_core, total, z_stage, recv_z,
    down_v, down_low, up_v, up_low, grad_v, down_sum, grad_wide, hid_wide,
    hid_part, hid_core, hid_half, hid_far, hid_low,
    grad_part, grad_x, grad_y, grad_z, grad_low,
    up_part, up_core, up_half, up_far, up_sum,
    local_sem, send_sem, recv_sem, z_send, z_recv, core_send, core_recv, far_send, far_recv,
    small_send, small_recv,
):
    row = lax.axis_index("row")
    col = lax.axis_index("col")
    z_hi, core = row // 2, row % 2
    x, y, z_lo = col // 8, (col // 2) % 4, col % 2
    contract_last = (((1,), (1,)), ((), ()))
    contract_first = (((0,), (0,)), ((), ()))

    def base(piece):
        dx, dy, dz, kind = piece
        return ((x + dx) % 4 * 8 + (y + dy) % 4 * 2 + (z_lo + dz) % 2) * SHARD + kind * PIECE

    def neighbour(axis, way):
        if axis == 0:
            return (row, (x + way) % 4 * 8 + y * 2 + z_lo)
        return (row, x * 8 + (y + way) % 4 * 2 + z_lo)

    z_mate = (row, x * 8 + y * 2 + 1 - z_lo)
    core_mate = (z_hi * 2 + 1 - core, col)
    far_mate = ((1 - z_hi) * 2 + core, col)

    loads = [
        pltpu.make_async_copy(source, target, local_sem.at[at])
        for at, (source, target) in enumerate((
            (x_ref, xg.at[pl.ds(pl.multiple_of(col * SHARD, SHARD), SHARD)]),
            (down_ref, down_v), (up_ref, up_v), (grad_ref, grad_v), (w_ref, w_v),
        ))
    ]
    for load in loads:
        load.start()
    own, down_load, up_load, grad_load, weight_load = loads

    barrier = pltpu.get_barrier_semaphore()
    mates = [neighbour(axis, way) for axis in (0, 1) for way in (1, 2, 3)] + [z_mate, core_mate, far_mate]
    for mate in mates:
        pl.semaphore_signal(barrier, inc=1, device_id=mate, device_id_type=MESH)
    pl.semaphore_wait(barrier, len(mates))
    own.wait()

    def remote(start, rows, ssem, rsem, mate):
        spot = xg.at[pl.ds(pl.multiple_of(start, HALF), rows)]
        return pltpu.make_async_remote_copy(
            src_ref=spot, dst_ref=spot, send_sem=ssem, recv_sem=rsem, device_id=mate, device_id_type=MESH
        )

    def sending(axis, way, item):
        name, zz = item[0], item[-1]
        kind = axis if name in ("F", "RF") else 1 - axis
        back = 3 if way == 0 else 1
        if name == "F":
            start, rows = base(offsets(kind, 0, 0, zz)), PIECE
        elif name == "RF":
            start, rows = base(offsets(kind, back, 0, zz)) + way * HALF, HALF
        elif name == "L":
            start, rows = base(offsets(kind, item[1], 0, zz)), PIECE
        else:
            start, rows = base(offsets(kind, item[1], back, zz)) + way * HALF, HALF
        at = ITEMS.index(item)
        return remote(
            start, rows, send_sem.at[axis, way, at], recv_sem.at[axis, way, at],
            neighbour(axis, 1 if way == 0 else 3),
        )

    def receiving(axis, way, item):
        pieces = landed(axis, item)
        if len(pieces) == 2:
            start, rows = base(pieces[way]), PIECE
        else:
            start, rows = base(pieces[0]) + way * HALF, HALF
        at = ITEMS.index(item)
        return remote(
            start, rows, send_sem.at[axis, way, at], recv_sem.at[axis, way, at],
            neighbour(axis, 1 if way == 0 else 3),
        )

    def every(step, action):
        for item in STEPS[step]:
            for axis in (0, 1):
                for way in (0, 1):
                    action(axis, way, item)

    def send(step):
        every(step, lambda *what: sending(*what).start())

    def arrive(step):
        every(step, lambda *what: receiving(*what).wait_recv())

    def z_copy(kind, dz):
        return remote(base((0, 0, dz, kind)), PIECE, z_send.at[kind], z_recv.at[kind], z_mate)

    send(0)
    for kind in (0, 1):
        z_copy(kind, 0).start()
    send(1)

    def small(name, source, target, mate):
        at = SMALL.index(name)
        return pltpu.make_async_remote_copy(
            src_ref=source, dst_ref=target, send_sem=small_send.at[at], recv_sem=small_recv.at[at],
            device_id=mate, device_id_type=MESH,
        )

    half = pl.ds(core * (TRIALS // 2), TRIALS // 2)
    other_half = pl.ds((1 - core) * (TRIALS // 2), TRIALS // 2)
    sends = {
        "hid_core": lambda: small("hid_core", hid_part, hid_core, core_mate),
        "hid_far": lambda: small("hid_far", hid_half, hid_far, far_mate),
        "hid_z": lambda: small("hid_z", hid_low.at[col], hid_low.at[col], z_mate),
        "grad_z": lambda: small("grad_z", grad_z.at[z_lo], grad_z.at[z_lo], z_mate),
        "low_core": lambda: small(
            "low_core", grad_low.at[pl.ds(row * 4, 4)], grad_low.at[pl.ds(row * 4, 4)], core_mate),
        "low_far": lambda: small(
            "low_far", grad_low.at[pl.ds(z_hi * 8, 8)], grad_low.at[pl.ds(z_hi * 8, 8)], far_mate),
        "up_core": lambda: small("up_core", up_part.at[other_half], up_core, core_mate),
        "up_far": lambda: small("up_far", up_half, up_far, far_mate),
        "up_share": lambda: small("up_share", up_sum.at[half], up_sum.at[half], core_mate),
    }
    for way in (1, 2, 3):
        def along(way=way):
            to_x, to_y = neighbour(0, way), neighbour(1, way)
            block, plane = pl.ds(x * 8 + y * 2, 2), pl.ds(x * 8, 8)
            sends[f"hid_y{way}"] = lambda: small(f"hid_y{way}", hid_low.at[block], hid_low.at[block], to_y)
            sends[f"hid_x{way}"] = lambda: small(f"hid_x{way}", hid_low.at[plane], hid_low.at[plane], to_x)
            sends[f"grad_x{way}"] = lambda: small(
                f"grad_x{way}", grad_part.at[(x + way) % 4], grad_x.at[x], to_x)
            sends[f"grad_y{way}"] = lambda: small(f"grad_y{way}", grad_y.at[y], grad_y.at[y], to_y)
            own_chunk = row * 4 + x
            sends[f"low_x{way}"] = lambda: small(
                f"low_x{way}", grad_low.at[own_chunk], grad_low.at[own_chunk], to_x)
        along()

    def go(*names):
        for name in names:
            sends[name]().start()

    def come(*names):
        for name in names:
            sends[name]().wait_recv()

    def trio(name):
        return [f"{name}{way}" for way in (1, 2, 3)]

    def bounds(shape, axis):
        label = lax.broadcasted_iota(jnp.int32, shape, axis) // RANK
        low, high = jnp.zeros(shape, jnp.int32), jnp.zeros(shape, jnp.int32)
        first = jnp.zeros((1, 1), jnp.int32)
        for trial in range(TRIALS):
            count = jnp.sum((trial_ref[...] <= trial).astype(jnp.int32), keepdims=True)
            low = jnp.where(label == trial, first, low)
            high = jnp.where(label == trial, count, high)
            first = count
        return low, high

    lane_low, lane_high = bounds((1, FLAT), 1)
    side_low, side_high = bounds((FLAT, 1), 0)
    spread = (
        lax.broadcasted_iota(jnp.int32, (RANK, FLAT), 1) % RANK
        == lax.broadcasted_iota(jnp.int32, (RANK, FLAT), 0)
    ).astype(jnp.bfloat16)

    def pick_rank(full, start):
        rows = full.shape[1]
        where = start + lax.broadcasted_iota(jnp.int32, (FLAT, rows), 1)
        mine = jnp.where((where >= side_low) & (where < side_high), full, 0.0)
        return jnp.sum(mine.reshape(TRIALS, RANK, rows), axis=0)

    def widen(low, start):
        values = lax.dot_general(low, spread, contract_first, preferred_element_type=jnp.float32)
        where = start + lax.broadcasted_iota(jnp.int32, values.shape, 0)
        return jnp.where((where >= lane_low) & (where < lane_high), values, 0.0).astype(jnp.bfloat16)

    down_load.wait()

    def cast_down(trial, carry):
        down_low[pl.ds(pl.multiple_of(trial * RANK, RANK), RANK), :] = down_v[trial].astype(jnp.bfloat16)
        return carry

    lax.fori_loop(0, TRIALS, cast_down, 0)
    own_rows = xg[pl.ds(pl.multiple_of(col * SHARD, SHARD), SHARD), :]
    hid_part[...] = pick_rank(
        lax.dot_general(down_low[...], own_rows, contract_last, preferred_element_type=jnp.float32), col * SHARD
    )
    go("hid_core")

    down_sum[...] = jnp.zeros_like(down_sum)
    total[...] = jnp.zeros_like(total)
    weight_load.wait()

    def hid_0():
        come("hid_core")
        hid_half[...] = hid_part[...] + hid_core[...]
        go("hid_far")

    def hid_1():
        come("hid_far")
        hid_low[col] = ((hid_half[...] + hid_far[...]) * INV_WIDTH).astype(jnp.bfloat16)
        go("hid_z")

    def hid_2():
        come("hid_z")
        go(*trio("hid_y"))

    def hid_3():
        come(*trio("hid_y"))

        @pl.when(x == row)
        def _():
            go(*trio("hid_x"))

    def hid_4():
        for way in (1, 2, 3):
            @pl.when((x - way + 4) % 4 == row)
            def _():
                sends[f"hid_x{way}"]().wait_recv()

    def grad_0():
        up_load.wait()
        for trial in range(TRIALS):
            up_low[trial * RANK:(trial + 1) * RANK, :] = up_v[trial].astype(jnp.bfloat16)
        grad_load.wait()

        def gradient_chunk(chunk, carry):
            start = pl.multiple_of(chunk * 256, 256)
            full = lax.dot_general(
                up_low[...], grad_v[pl.ds(start, 256), :], contract_last, preferred_element_type=jnp.float32
            )
            grad_part[chunk] = pick_rank(full, row * 8 * SHARD + start)
            return carry

        lax.fori_loop(0, 4, gradient_chunk, 0)
        grad_x[x] = grad_part[x]

    def grad_1():
        go(*trio("grad_x"))

    def grad_2():
        come(*trio("grad_x"))
        grad_y[y] = (grad_x[0] + grad_x[1]) + (grad_x[2] + grad_x[3])
        go(*trio("grad_y"))

    def grad_3():
        come(*trio("grad_y"))
        grad_z[z_lo] = (grad_y[0] + grad_y[1]) + (grad_y[2] + grad_y[3])
        go("grad_z")

    def grad_4():
        come("grad_z")
        grad_low[row * 4 + x] = ((grad_z[0] + grad_z[1]) * SCALE).astype(jnp.bfloat16)
        go(*trio("low_x"))

    def grad_5():
        come(*trio("low_x"))
        go("low_core")

    def grad_6():
        come("low_core")
        go("low_far")

    def grad_7():
        come("low_far")

        def wide(chunk, carry):
            start = pl.multiple_of(chunk * 256, 256)
            grad_wide[pl.ds(start, 256), :] = widen(grad_low[chunk], start)
            return carry

        lax.fori_loop(0, 16, wide, 0)

    def up_0():
        def wide(block, carry):
            start = pl.multiple_of(block * SHARD, SHARD)
            hid_wide[pl.ds(start, SHARD), :] = widen(hid_low[row * 8 + block], row * 8 * SHARD + start)
            return carry

        lax.fori_loop(0, 8, wide, 0)
        full = lax.dot_general(hid_wide[...], grad_v[...], contract_first, preferred_element_type=jnp.float32)
        up_part[...] = full.reshape(up_part.shape)
        go("up_core")

    def up_1():
        come("up_core")
        up_half[...] = up_part[half] + up_core[...]
        go("up_far")

    def up_2():
        come("up_far")
        up_sum[half] = up_half[...] + up_far[...]
        go("up_share")

    def up_3():
        come("up_share")

        def moved(slot, carry):
            trial = keeper_ref[slot]
            new_up_ref[slot] = up_v[trial] - rate_ref[trial] * (up_sum[trial] * SCALE)
            return carry

        lax.fori_loop(0, TRIALS, moved, 0)

    def adapter_term():
        def adapter(block, carry):
            spot = pl.ds(pl.multiple_of(block * SHARD, SHARD), SHARD)
            total[spot, :] += SCALE * jnp.dot(
                hid_wide[spot, :], up_low[...], preferred_element_type=jnp.float32
            )
            return carry

        lax.fori_loop(0, 8, adapter, 0)

    ahead = {0: [hid_0], 1: [hid_1, grad_1], 2: [hid_2], 3: [grad_2], 4: [hid_3], 5: [grad_3], 6: [hid_4, grad_4],
             7: [up_1], 8: [grad_5], 9: [up_2, grad_6]}
    after = {0: [grad_0], 6: [up_0], 8: [adapter_term], 10: [up_3], 11: [grad_7]}

    def decode(code):
        dx, dy, dz, kind = code % 4, code // 4 % 4, code // 16 % 2, code // 32
        return (x + dx) % 4, base((dx, dy, dz, kind))

    def core_copy(slot):
        return pltpu.make_async_remote_copy(
            src_ref=stage.at[slot], dst_ref=recv_core.at[slot],
            send_sem=core_send.at[slot], recv_sem=core_recv.at[slot],
            device_id=core_mate, device_id_type=MESH,
        )

    def far_copy(number):
        spot = pl.ds(pl.multiple_of(number * PIECE, PIECE), PIECE)
        return pltpu.make_async_remote_copy(
            src_ref=z_stage.at[spot], dst_ref=recv_z.at[spot],
            send_sem=far_send.at[number], recv_sem=far_recv.at[number],
            device_id=far_mate, device_id_type=MESH,
        )

    def group_places(group):
        return [decode(select(group, [codes[slot] for codes in CODES])) for slot in range(4)]

    def group_rows(places):
        starts = [pl.multiple_of(start, PIECE) for _, start in places]
        return starts, jnp.concatenate([xg[pl.ds(start, PIECE), :] for start in starts], axis=0)

    def add_down(starts, rows):
        wide = jnp.concatenate([grad_wide[pl.ds(start, PIECE), :] for start in starts], axis=0)
        down_sum[...] += lax.dot_general(
            wide, rows, contract_first, preferred_element_type=jnp.float32
        ).reshape(down_sum.shape)

    def finish(group):
        places = group_places(group)
        for slot in range(4):
            plane, start = places[slot]

            @pl.when(plane == row)
            def _():
                number = start % (8 * SHARD) // PIECE
                far_copy(number).wait_recv()
                spot = pl.ds(pl.multiple_of(number * PIECE, PIECE), PIECE)
                proj_ref[spot, :] = (total[spot, :] + recv_z[spot, :].astype(jnp.float32)).astype(jnp.bfloat16)

    def body(group, carry):
        @pl.when(group > 0)
        def _():
            past = group - 1
            places = group_places(past)
            for pair in (0, 1):
                @pl.when(places[2 * pair][0] % 2 == core)
                def _():
                    slot = select(past, [slots[pair] for slots in SLOTS])
                    core_copy(slot).wait_recv()
                    for part in (0, 1):
                        plane, start = places[2 * pair + part]
                        number = start % (8 * SHARD) // PIECE
                        spot = pl.ds(pl.multiple_of(number * PIECE, PIECE), PIECE)
                        summed = (
                            keep[past % 2, pl.ds((2 * pair + part) * PIECE, PIECE), :]
                            + recv_core[slot, part * PIECE:(part + 1) * PIECE, :].astype(jnp.float32)
                        )

                        @pl.when(plane // 2 == z_hi)
                        def _():
                            total[spot, :] += summed

                        @pl.when(plane // 2 != z_hi)
                        def _():
                            z_stage[spot, :] = summed.astype(jnp.bfloat16)
                            far_copy(number).start()

        @pl.when(group == Z_GROUP)
        def _():
            for work in ahead.get(Z_GROUP, ()):
                work()

        for step in range(len(STEPS)):
            @pl.when(group == (step if step < Z_GROUP else step + 1))
            def _():
                arrive(step)
                if step == Z_GROUP - 1:
                    for kind in (0, 1):
                        z_copy(kind, 1).wait_recv()
                for work in ahead.get(step if step < Z_GROUP else step + 1, ()):
                    work()
                if step + 2 < len(STEPS):
                    send(step + 2)

        @pl.when(group < GROUPS)
        def _():
            places = group_places(group)
            starts, rows = group_rows(places)
            product = jnp.dot(rows, w_v[...], preferred_element_type=jnp.float32)
            keep[group % 2] = product
            for pair in (0, 1):
                @pl.when(places[2 * pair][0] % 2 != core)
                def _():
                    slot = select(group, [slots[pair] for slots in SLOTS])
                    stage[slot] = product[pair * 2 * PIECE:(pair + 1) * 2 * PIECE].astype(jnp.bfloat16)
                    core_copy(slot).start()

        for at, works in after.items():
            @pl.when(group == at)
            def _():
                for work in works:
                    work()

        @pl.when((group >= CATCH_UP) & (group < GROUPS))
        def _():
            add_down(*group_rows(group_places(group)))

            def earlier(number, carry):
                before = (group - CATCH_UP) * 3 + number

                @pl.when(before < CATCH_UP)
                def _():
                    add_down(*group_rows(group_places(before)))

                return carry

            lax.fori_loop(0, 3, earlier, 0)

        @pl.when(group >= FINISH)
        def _():
            finish(group - FINISH_LAG)

        @pl.when((group >= FINISH) & (group < 2 * FINISH - FINISH_LAG))
        def _():
            finish(group - FINISH)

        return carry

    lax.fori_loop(0, GROUPS + 1, body, 0)

    def moved_down(slot, carry):
        trial = keeper_ref[slot]
        new_down_ref[slot] = down_v[trial] - rate_ref[trial] * (down_sum[trial] * INV_WIDTH)
        return carry

    lax.fori_loop(0, TRIALS, moved_down, 0)

    def last(group, carry):
        finish(group)
        return carry

    lax.fori_loop(GROUPS - FINISH_LAG + 1, GROUPS, last, 0)

    for step in range(len(STEPS)):
        every(step, lambda *what: sending(*what).wait_send())
    for kind in (0, 1):
        z_copy(kind, 0).wait_send()
    for name in SMALL:
        if not name.startswith("hid_x"):
            sends[name]().wait_send()

    @pl.when(x == row)
    def _():
        for name in trio("hid_x"):
            sends[name]().wait_send()

    def drain(number, carry):
        far_copy(number).wait_send()
        core_copy(number).wait_send()
        return carry

    lax.fori_loop(0, 16, drain, 0)


def write_out(*refs):
    sources, targets, sems = refs[:3], refs[3:6], refs[6]
    copies = [pltpu.make_async_copy(sources[at], targets[at], sems.at[at]) for at in range(3)]
    for copy in copies:
        copy.start()
    for copy in copies:
        copy.wait()


def per_device(
    packed_input_rows,
    frozen_weight,
    down_adapters,
    up_adapters,
    trial_learning_rates,
    row_trial_index,
    output_gradient,
    keeper_slot,
):
    width_in, width_out = frozen_weight.shape
    all_rows = row_trial_index.shape[0]
    block_rows = output_gradient.shape[0]
    vmem = pl.BlockSpec(memory_space=pltpu.VMEM)
    smem = pl.BlockSpec(memory_space=pltpu.SMEM)
    hbm = pl.BlockSpec(memory_space=pl.ANY)
    dma = pltpu.SemaphoreType.DMA
    f32, bf16 = jnp.float32, jnp.bfloat16
    half = TRIALS // 2
    held = pl.pallas_call(
        whole_kernel,
        name="adapter_sweep",
        out_shape=(
            pltpu.VMEM((block_rows, width_out), bf16),
            pltpu.VMEM(down_adapters.shape, f32),
            pltpu.VMEM(up_adapters.shape, f32),
        ),
        in_specs=[hbm, hbm, hbm, hbm, smem, vmem, hbm, smem],
        out_specs=(vmem, vmem, vmem),
        scratch_shapes=[
            pltpu.VMEM((all_rows, width_in), bf16),
            pltpu.VMEM((width_in, width_out), bf16),
            pltpu.VMEM((2, 4 * PIECE, width_out), f32),
            pltpu.VMEM((PAIRS, 2 * PIECE, width_out), bf16),
            pltpu.VMEM((PAIRS, 2 * PIECE, width_out), bf16),
            pltpu.VMEM((block_rows, width_out), f32),
            pltpu.VMEM((block_rows, width_out), bf16),
            pltpu.VMEM((block_rows, width_out), bf16),
            pltpu.VMEM(down_adapters.shape, f32),
            pltpu.VMEM((FLAT, width_in), bf16),
            pltpu.VMEM(up_adapters.shape, f32),
            pltpu.VMEM((FLAT, width_out), bf16),
            pltpu.VMEM((block_rows, width_out), bf16),
            pltpu.VMEM(down_adapters.shape, f32),
            pltpu.VMEM((all_rows, FLAT), bf16),
            pltpu.VMEM((block_rows, FLAT), bf16),
            pltpu.VMEM((RANK, SHARD), f32),
            pltpu.VMEM((RANK, SHARD), f32),
            pltpu.VMEM((RANK, SHARD), f32),
            pltpu.VMEM((RANK, SHARD), f32),
            pltpu.VMEM((32, RANK, SHARD), bf16),
            pltpu.VMEM((4, RANK, 256), f32),
            pltpu.VMEM((4, RANK, 256), f32),
            pltpu.VMEM((4, RANK, 256), f32),
            pltpu.VMEM((2, RANK, 256), f32),
            pltpu.VMEM((16, RANK, 256), bf16),
            pltpu.VMEM((TRIALS, RANK, width_out), f32),
            pltpu.VMEM((half, RANK, width_out), f32),
            pltpu.VMEM((half, RANK, width_out), f32),
            pltpu.VMEM((half, RANK, width_out), f32),
            pltpu.VMEM((TRIALS, RANK, width_out), f32),
            dma((5,)),
            dma((2, 2, len(ITEMS))),
            dma((2, 2, len(ITEMS))),
            dma((2,)),
            dma((2,)),
            dma((PAIRS,)),
            dma((PAIRS,)),
            dma((16,)),
            dma((16,)),
            dma((len(SMALL),)),
            dma((len(SMALL),)),
        ],
        compiler_params=pltpu.CompilerParams(
            collective_id=0, has_side_effects=True, vmem_limit_bytes=56 << 20
        ),
        cost_estimate=pl.CostEstimate(flops=22 * 10**9, bytes_accessed=20 << 20, transcendentals=0),
    )(
        packed_input_rows, frozen_weight, down_adapters, up_adapters, trial_learning_rates,
        row_trial_index.reshape(32, all_rows // 32), output_gradient, keeper_slot,
    )
    held = [pltpu.with_memory_space_constraint(array, pltpu.VMEM) for array in held]
    return tuple(pl.pallas_call(
        write_out,
        name="write_out",
        out_shape=tuple(jax.ShapeDtypeStruct(array.shape, array.dtype) for array in held),
        in_specs=[vmem] * len(held),
        out_specs=tuple([hbm] * len(held)),
        scratch_shapes=[dma((len(held),))],
        compiler_params=pltpu.CompilerParams(vmem_limit_bytes=1 << 20),
    )(*held))


def solution(mesh):
    in_specs = (
        P("col", "row"),
        P("row", "col"),
        P(None, None, "row"),
        P(None, None, "col"),
        P(),
        P(),
        P("row", "col"),
        P(),
    )
    out_specs = (P("row", "col"), P(None, None, "row"), P(None, None, "col"))
    return jax.shard_map(
        per_device, mesh=mesh, in_specs=in_specs, out_specs=out_specs, check_vma=False
    )
```

```python
import jax
import jax.numpy as jnp
from jax import lax
from jax.experimental import pallas as pl
from jax.experimental.pallas import tpu as pltpu
from jax.sharding import PartitionSpec as P

MESH = pl.DeviceIdType.MESH
D = 8192
RANK = 16
TRIALS = 16
FLAT = RANK * TRIALS
SHARD = 128
PIECE = 64
HALF = 32
SCALE = 2.0 / RANK
INV_WIDTH = D ** (-0.5)

STEPS = (
    (
        (("F", 0),),
        (("L", 0, 0),),
        (("L", 1, 0),),
        (("RF", 0), ("RL", 0, 0)),
        (("L", 3, 0),),
        (("L", 0, 1),),
        (("L", 2, 0),),
        (("F", 1),),
        (("RL", 1, 0), ("RL", 3, 0)),
        (("L", 2, 1),),
        (("L", 3, 1),),
        (("RL", 0, 1), ("RL", 2, 0)),
        (("L", 1, 1),),
        (("RL", 2, 1), ("RL", 3, 1)),
        (("RL", 1, 1),),
    ),
    (
        (("F", 0),),
        (("L", 0, 0),),
        (("L", 1, 0),),
        (("RF", 0), ("RL", 0, 0)),
        (("L", 3, 0),),
        (("L", 0, 1),),
        (("L", 2, 0),),
        (("F", 1),),
        (("RL", 1, 0), ("RL", 3, 0)),
        (("L", 2, 1),),
        (("L", 1, 1),),
        (("RL", 2, 0), ("RL", 2, 1)),
        (("L", 3, 1),),
        (("RL", 0, 1), ("RL", 1, 1)),
        (("RL", 3, 1),),
    ),
)
ITEMS = tuple(item for step in STEPS[0] for item in step)
COUNT = len(STEPS[0])
SWAP_SENT, SWAP_USED = 2, 5
Z_GROUP = 3
GROUPS = COUNT
TURN = [step + (step >= Z_GROUP) for step in range(COUNT)]


def offsets(kind, first, last, zz):
    return (first, last, zz, 0) if kind == 0 else (last, first, zz, 1)


def landed(axis, item):
    name, zz = item[0], item[-1]
    kind = axis if name in ("F", "RF") else 1 - axis
    if name == "F":
        return [offsets(kind, 3, 0, zz), offsets(kind, 2 if zz else 1, 0, zz)]
    if name == "RF":
        return [offsets(kind, 2, 0, zz)]
    if name == "L":
        return [offsets(kind, item[1], 3, zz), offsets(kind, item[1], 1, zz)]
    return [offsets(kind, item[1], 2, zz)]


def group_pieces():
    groups = []
    for step in range(COUNT):
        groups.append([
            piece for axis in (0, 1) for item in STEPS[axis][step] for piece in landed(axis, item)
        ])
    groups.insert(Z_GROUP, [(0, 0, 0, 0), (0, 0, 1, 0), (0, 0, 0, 1), (0, 0, 1, 1)])
    groups[-1] = [offsets(kind, 1, 0, 1) for kind in (0, 1)] + groups[-1]
    return groups


CODES = [[dx + 4 * dy + 16 * dz + 32 * kind for dx, dy, dz, kind in group] for group in group_pieces()]


def piece_slots():
    seen, slots = [0, 0], []
    for group in group_pieces():
        slots.append([])
        for piece in group:
            odd = piece[0] % 2
            slots[-1].append(seen[odd])
            seen[odd] += 1
    return slots


SLOTS = piece_slots()
SENT = 32
SMALL = (
    ["hid_core", "hid_far", "hid_z"] + [f"hid_y{k}" for k in (1, 2, 3)] + [f"hid_x{k}" for k in (1, 2, 3)]
    + [f"grad_x{k}" for k in (1, 2, 3)] + [f"grad_y{k}" for k in (1, 2, 3)] + ["grad_z"]
    + [f"low_x{k}" for k in (1, 2, 3)] + ["low_core", "low_far", "up_core", "up_far", "up_share"]
)
FINISH, FINISH_LAG = 10, 5
CATCH_UP, CATCH_EACH = 11, 2


def select(index, values):
    out = jnp.int32(values[0])
    for at in range(1, len(values)):
        out = jnp.where(index == at, jnp.int32(values[at]), out)
    return out


def whole_kernel(
    x_ref, w_ref, down_ref, up_ref, rate_ref, trial_ref, grad_ref, keeper_ref,
    proj_ref, new_down_ref, new_up_ref,
    xg, w_v, keep, keep_half, stage, recv_core, total, z_stage, recv_z,
    down_v, down_low, up_v, up_low, grad_v, down_sum, grad_wide, hid_wide,
    hid_part, hid_core, hid_half, hid_far, hid_low,
    grad_part, grad_sum, grad_x, grad_y, grad_z, grad_low,
    up_part, up_core, up_half, up_far, up_sum,
    local_sem, send_sem, recv_sem, z_send, z_recv, swap_send, swap_recv, core_send, core_recv, far_send, far_recv,
    small_send, small_recv,
):
    row = lax.axis_index("row")
    col = lax.axis_index("col")
    z_hi, core = row // 2, row % 2
    x, y, z_lo = col // 8, (col // 2) % 4, col % 2
    contract_last = (((1,), (1,)), ((), ()))
    contract_first = (((0,), (0,)), ((), ()))

    def base(piece):
        dx, dy, dz, kind = piece
        return ((x + dx) % 4 * 8 + (y + dy) % 4 * 2 + (z_lo + dz) % 2) * SHARD + kind * PIECE

    def neighbour(axis, way):
        if axis == 0:
            return (row, (x + way) % 4 * 8 + y * 2 + z_lo)
        return (row, x * 8 + (y + way) % 4 * 2 + z_lo)

    z_mate = (row, x * 8 + y * 2 + 1 - z_lo)
    core_mate = (z_hi * 2 + 1 - core, col)
    far_mate = ((1 - z_hi) * 2 + core, col)

    loads = [
        pltpu.make_async_copy(source, target, local_sem.at[at])
        for at, (source, target) in enumerate((
            (x_ref, xg.at[pl.ds(pl.multiple_of(col * SHARD, SHARD), SHARD)]),
            (down_ref, down_v), (up_ref, up_v), (grad_ref, grad_v), (w_ref, w_v),
        ))
    ]
    for load in loads:
        load.start()
    own, down_load, up_load, grad_load, weight_load = loads

    barrier = pltpu.get_barrier_semaphore()
    mates = [neighbour(axis, way) for axis in (0, 1) for way in (1, 2, 3)] + [z_mate, core_mate, far_mate]
    for mate in mates:
        pl.semaphore_signal(barrier, inc=1, device_id=mate, device_id_type=MESH)
    pl.semaphore_wait(barrier, len(mates))
    own.wait()

    def remote(start, rows, ssem, rsem, mate):
        spot = xg.at[pl.ds(pl.multiple_of(start, HALF), rows)]
        return pltpu.make_async_remote_copy(
            src_ref=spot, dst_ref=spot, send_sem=ssem, recv_sem=rsem, device_id=mate, device_id_type=MESH
        )

    def sending(axis, way, item):
        name, zz = item[0], item[-1]
        kind = axis if name in ("F", "RF") else 1 - axis
        back = 3 if way == 0 else 1
        if name == "F":
            start, rows = base(offsets(kind, way if zz else 0, 0, zz)), PIECE
        elif name == "RF":
            start, rows = base(offsets(kind, back, 0, zz)) + way * HALF, HALF
        elif name == "L":
            start, rows = base(offsets(kind, item[1], 0, zz)), PIECE
        else:
            start, rows = base(offsets(kind, item[1], back, zz)) + way * HALF, HALF
        at = ITEMS.index(item)
        return remote(
            start, rows, send_sem.at[axis, way, at], recv_sem.at[axis, way, at],
            neighbour(axis, 1 if way == 0 else 3),
        )

    def receiving(axis, way, item):
        pieces = landed(axis, item)
        if len(pieces) == 2:
            start, rows = base(pieces[way]), PIECE
        else:
            start, rows = base(pieces[0]) + way * HALF, HALF
        at = ITEMS.index(item)
        return remote(
            start, rows, send_sem.at[axis, way, at], recv_sem.at[axis, way, at],
            neighbour(axis, 1 if way == 0 else 3),
        )

    def every(step, action):
        for axis in (0, 1):
            for item in STEPS[axis][step]:
                for way in (0, 1):
                    action(axis, way, item)

    def send(step):
        every(step, lambda *what: sending(*what).start())

    def arrive(step):
        every(step, lambda *what: receiving(*what).wait_recv())

    def z_copy(kind, dz):
        return remote(base((0, 0, dz, kind)), PIECE, z_send.at[kind], z_recv.at[kind], z_mate)

    def swap(kind, dz):
        return remote(base(offsets(kind, 1, 0, dz)), PIECE, swap_send.at[kind], swap_recv.at[kind], z_mate)

    send(0)
    for kind in (0, 1):
        z_copy(kind, 0).start()
    send(1)

    def small(name, source, target, mate):
        at = SMALL.index(name)
        return pltpu.make_async_remote_copy(
            src_ref=source, dst_ref=target, send_sem=small_send.at[at], recv_sem=small_recv.at[at],
            device_id=mate, device_id_type=MESH,
        )

    half = pl.ds(core * (TRIALS // 2), TRIALS // 2)
    other_half = pl.ds((1 - core) * (TRIALS // 2), TRIALS // 2)
    sends = {
        "hid_core": lambda: small("hid_core", hid_part, hid_core, core_mate),
        "hid_far": lambda: small("hid_far", hid_half, hid_far, far_mate),
        "hid_z": lambda: small("hid_z", hid_low.at[col], hid_low.at[col], z_mate),
        "grad_z": lambda: small("grad_z", grad_part, grad_z, z_mate),
        "low_core": lambda: small(
            "low_core", grad_low.at[pl.ds(row * 4, 4)], grad_low.at[pl.ds(row * 4, 4)], core_mate),
        "low_far": lambda: small(
            "low_far", grad_low.at[pl.ds(z_hi * 8, 8)], grad_low.at[pl.ds(z_hi * 8, 8)], far_mate),
        "up_core": lambda: small("up_core", up_part.at[other_half], up_core, core_mate),
        "up_far": lambda: small("up_far", up_half, up_far, far_mate),
        "up_share": lambda: small("up_share", up_sum.at[half], up_sum.at[half], core_mate),
    }
    for way in (1, 2, 3):
        def along(way=way):
            to_x, to_y = neighbour(0, way), neighbour(1, way)
            block, plane = pl.ds(x * 8 + y * 2, 2), pl.ds(x * 8, 8)
            sends[f"hid_y{way}"] = lambda: small(f"hid_y{way}", hid_low.at[block], hid_low.at[block], to_y)
            sends[f"hid_x{way}"] = lambda: small(f"hid_x{way}", hid_low.at[plane], hid_low.at[plane], to_x)
            sends[f"grad_x{way}"] = lambda: small(
                f"grad_x{way}", grad_sum.at[(x + way) % 4], grad_x.at[x], to_x)
            sends[f"grad_y{way}"] = lambda: small(f"grad_y{way}", grad_y.at[y], grad_y.at[y], to_y)
            own_chunk = row * 4 + x
            sends[f"low_x{way}"] = lambda: small(
                f"low_x{way}", grad_low.at[own_chunk], grad_low.at[own_chunk], to_x)
        along()

    def go(*names):
        for name in names:
            sends[name]().start()

    def come(*names):
        for name in names:
            sends[name]().wait_recv()

    def trio(name):
        return [f"{name}{way}" for way in (1, 2, 3)]

    def bounds(shape, axis):
        label = lax.broadcasted_iota(jnp.int32, shape, axis) // RANK
        low, high = jnp.zeros(shape, jnp.int32), jnp.zeros(shape, jnp.int32)
        first = jnp.zeros((1, 1), jnp.int32)
        for trial in range(TRIALS):
            count = jnp.sum((trial_ref[...] <= trial).astype(jnp.int32), keepdims=True)
            low = jnp.where(label == trial, first, low)
            high = jnp.where(label == trial, count, high)
            first = count
        return low, high

    lane_low, lane_high = bounds((1, FLAT), 1)
    side_low, side_high = bounds((FLAT, 1), 0)
    spread = (
        lax.broadcasted_iota(jnp.int32, (RANK, FLAT), 1) % RANK
        == lax.broadcasted_iota(jnp.int32, (RANK, FLAT), 0)
    ).astype(jnp.bfloat16)

    def pick_rank(full, start):
        rows = full.shape[1]
        where = start + lax.broadcasted_iota(jnp.int32, (FLAT, rows), 1)
        mine = jnp.where((where >= side_low) & (where < side_high), full, 0.0)
        return jnp.sum(mine.reshape(TRIALS, RANK, rows), axis=0)

    def widen(low, start):
        values = lax.dot_general(low, spread, contract_first, preferred_element_type=jnp.float32)
        where = start + lax.broadcasted_iota(jnp.int32, values.shape, 0)
        return jnp.where((where >= lane_low) & (where < lane_high), values, 0.0).astype(jnp.bfloat16)

    down_load.wait()

    def cast_down(trial, carry):
        down_low[pl.ds(pl.multiple_of(trial * RANK, RANK), RANK), :] = down_v[trial].astype(jnp.bfloat16)
        return carry

    lax.fori_loop(0, TRIALS, cast_down, 0)
    own_rows = xg[pl.ds(pl.multiple_of(col * SHARD, SHARD), SHARD), :]
    hid_part[...] = pick_rank(
        lax.dot_general(down_low[...], own_rows, contract_last, preferred_element_type=jnp.float32), col * SHARD
    )
    go("hid_core")

    down_sum[...] = jnp.zeros_like(down_sum)
    total[...] = jnp.zeros_like(total)
    weight_load.wait()

    def hid_0():
        come("hid_core")
        hid_half[...] = hid_part[...] + hid_core[...]
        go("hid_far")

    def hid_1():
        come("hid_far")
        hid_low[col] = ((hid_half[...] + hid_far[...]) * INV_WIDTH).astype(jnp.bfloat16)
        go("hid_z")

    def hid_2():
        come("hid_z")
        go(*trio("hid_y"))

    def hid_3():
        come(*trio("hid_y"))

        @pl.when(x == row)
        def _():
            go(*trio("hid_x"))

    def hid_4():
        for way in (1, 2, 3):
            @pl.when((x - way + 4) % 4 == row)
            def _():
                sends[f"hid_x{way}"]().wait_recv()

    def grad_0():
        up_load.wait()
        for trial in range(TRIALS):
            up_low[trial * RANK:(trial + 1) * RANK, :] = up_v[trial].astype(jnp.bfloat16)
        grad_load.wait()

        def gradient_chunk(chunk, carry):
            start = pl.multiple_of(chunk * 256, 256)
            full = lax.dot_general(
                up_low[...], grad_v[pl.ds(start, 256), :], contract_last, preferred_element_type=jnp.float32
            )
            grad_part[chunk] = pick_rank(full, row * 8 * SHARD + start)
            return carry

        lax.fori_loop(0, 4, gradient_chunk, 0)

    def grad_1():
        come("grad_z")
        grad_sum[...] = grad_part[...] + grad_z[...]
        go(*trio("grad_x"))
        grad_x[x] = grad_sum[x]

    def grad_2():
        come(*trio("grad_x"))
        grad_y[y] = (grad_x[0] + grad_x[1]) + (grad_x[2] + grad_x[3])
        go(*trio("grad_y"))

    def grad_3():
        come(*trio("grad_y"))
        gradient = (grad_y[0] + grad_y[1]) + (grad_y[2] + grad_y[3])
        grad_low[row * 4 + x] = (gradient * SCALE).astype(jnp.bfloat16)
        go(*trio("low_x"))

    def grad_4():
        come(*trio("low_x"))
        go("low_core")

    def grad_5():
        come("low_core")
        go("low_far")

    def widen_gradient(side):
        def wide(number, carry):
            chunk = side * 8 + number
            start = pl.multiple_of(chunk * 256, 256)
            grad_wide[pl.ds(start, 256), :] = widen(grad_low[chunk], start)
            return carry

        lax.fori_loop(0, 8, wide, 0)

    def grad_6():
        widen_gradient(z_hi)

    def grad_7():
        come("low_far")
        widen_gradient(1 - z_hi)

    def up_0():
        def wide(block, carry):
            start = pl.multiple_of(block * SHARD, SHARD)
            hid_wide[pl.ds(start, SHARD), :] = widen(hid_low[row * 8 + block], row * 8 * SHARD + start)
            return carry

        lax.fori_loop(0, 8, wide, 0)
        full = lax.dot_general(hid_wide[...], grad_v[...], contract_first, preferred_element_type=jnp.float32)
        up_part[...] = full.reshape(up_part.shape)
        go("up_core")

    def up_1():
        come("up_core")
        up_half[...] = (up_part[half] + up_core[...]).astype(jnp.bfloat16)
        go("up_far")

    def up_2():
        come("up_far")
        up_sum[half] = up_half[...].astype(jnp.float32) + up_far[...].astype(jnp.float32)
        go("up_share")

    def up_3():
        come("up_share")

        def moved(slot, carry):
            trial = keeper_ref[slot]
            new_up_ref[slot] = up_v[trial] - rate_ref[trial] * (up_sum[trial] * SCALE)
            return carry

        lax.fori_loop(0, TRIALS, moved, 0)

    def adapter_term():
        def adapter(block, carry):
            spot = pl.ds(pl.multiple_of(block * SHARD, SHARD), SHARD)
            total[spot, :] += SCALE * jnp.dot(
                hid_wide[spot, :], up_low[...], preferred_element_type=jnp.float32
            )
            return carry

        lax.fori_loop(0, 8, adapter, 0)

    ahead = {0: [hid_0], 2: [hid_1, grad_1], 4: [hid_2, grad_2], 6: [hid_3, grad_3], 8: [hid_4, grad_4],
             9: [up_1, grad_5], 11: [up_2]}
    after = {7: [], 8: [up_0], 9: [grad_6], 10: [adapter_term], 11: [grad_7], 12: [up_3]}
    grad_0()
    go("grad_z")

    def decode(code):
        dx, dy, dz, kind = code % 4, code // 4 % 4, code // 16 % 2, code // 32
        return (x + dx) % 4, base((dx, dy, dz, kind))

    def core_copy(slot):
        return pltpu.make_async_remote_copy(
            src_ref=stage.at[slot], dst_ref=recv_core.at[slot],
            send_sem=core_send.at[slot], recv_sem=core_recv.at[slot],
            device_id=core_mate, device_id_type=MESH,
        )

    def far_copy(number):
        spot = pl.ds(pl.multiple_of(number * PIECE, PIECE), PIECE)
        return pltpu.make_async_remote_copy(
            src_ref=z_stage.at[spot], dst_ref=recv_z.at[spot],
            send_sem=far_send.at[number], recv_sem=far_recv.at[number],
            device_id=far_mate, device_id_type=MESH,
        )

    def group_places(group):
        return [decode(select(group, [codes[slot] for codes in CODES])) for slot in range(4)]

    def group_rows(places):
        starts = [pl.multiple_of(start, PIECE) for _, start in places]
        return starts, jnp.concatenate([xg[pl.ds(start, PIECE), :] for start in starts], axis=0)

    def add_down(starts, rows):
        wide = jnp.concatenate([grad_wide[pl.ds(start, PIECE), :] for start in starts], axis=0)
        down_sum[...] += lax.dot_general(
            wide, rows, contract_first, preferred_element_type=jnp.float32
        ).reshape(down_sum.shape)

    def finish(group):
        places = group_places(group)
        for slot in range(4):
            plane, start = places[slot]

            @pl.when(plane == row)
            def _():
                number = start % (8 * SHARD) // PIECE
                far_copy(number).wait_recv()
                spot = pl.ds(pl.multiple_of(number * PIECE, PIECE), PIECE)
                proj_ref[spot, :] = (total[spot, :] + recv_z[spot, :].astype(jnp.float32)).astype(jnp.bfloat16)

    def add_core(place, own_sum, slot):
        plane, start = place
        number = start % (8 * SHARD) // PIECE
        spot = pl.ds(pl.multiple_of(number * PIECE, PIECE), PIECE)
        summed = own_sum + recv_core[slot].astype(jnp.float32)

        @pl.when(plane // 2 == z_hi)
        def _():
            total[spot, :] += summed

        @pl.when(plane // 2 != z_hi)
        def _():
            z_stage[spot, :] = summed.astype(jnp.bfloat16)
            far_copy(number).start()

    def hand_over(places, slots, product):
        for at, (plane, _) in enumerate(places):
            @pl.when(plane % 2 != core)
            def _():
                stage[slots[at]] = product[at * PIECE:(at + 1) * PIECE].astype(jnp.bfloat16)
                core_copy(slots[at]).start()

    def take_over(places, slots, own_sums):
        for at, place in enumerate(places):
            @pl.when(place[0] % 2 == core)
            def _():
                core_copy(slots[at]).wait_recv()
                add_core(place, own_sums[at * PIECE:(at + 1) * PIECE, :], slots[at])

    extra_places = group_places(GROUPS)

    def extra_product(part):
        places, slots = extra_places[2 * part:2 * part + 2], SLOTS[GROUPS][2 * part:2 * part + 2]
        _, rows = group_rows(places)
        product = jnp.dot(rows, w_v[...], preferred_element_type=jnp.float32)
        keep_half[...] = product
        hand_over(places, slots, product)

    def extra_sum(part):
        take_over(extra_places[2 * part:2 * part + 2], SLOTS[GROUPS][2 * part:2 * part + 2], keep_half)

    after[7].append(lambda: extra_product(0))
    after[8].insert(0, lambda: extra_sum(0))

    def body(group, carry):
        @pl.when(group == Z_GROUP)
        def _():
            for work in ahead.get(Z_GROUP, ()):
                work()

        for step in range(COUNT - 1):
            @pl.when(group == TURN[step])
            def _():
                arrive(step)
                if step == Z_GROUP - 1:
                    for kind in (0, 1):
                        z_copy(kind, 1).wait_recv()
                if step == SWAP_USED:
                    for kind in (0, 1):
                        swap(kind, 1).wait_recv()
                for work in ahead.get(TURN[step], ()):
                    work()
                if step + 2 < COUNT:
                    send(step + 2)
                if step == SWAP_SENT:
                    for kind in (0, 1):
                        swap(kind, 0).start()

        places = group_places(group)
        starts, rows = group_rows(places)
        product = jnp.dot(rows, w_v[...], preferred_element_type=jnp.float32)
        keep[...] = product
        slots = [select(group, [each[at] for each in SLOTS]) for at in range(4)]
        hand_over(places, slots, product)

        for at, works in after.items():
            @pl.when(group == at)
            def _():
                for work in works:
                    work()

        @pl.when(group >= CATCH_UP)
        def _():
            add_down(*group_rows(group_places(group)))

        take_over(places, slots, keep)

        @pl.when(group >= CATCH_UP)
        def _():
            def earlier(number, carry):
                add_down(*group_rows(group_places((group - CATCH_UP) * CATCH_EACH + number)))
                return carry

            lax.fori_loop(0, CATCH_EACH, earlier, 0)

        @pl.when(group >= FINISH)
        def _():
            finish(group - FINISH_LAG)
            finish(group - FINISH)

        return carry

    lax.fori_loop(0, GROUPS, body, 0)

    arrive(COUNT - 1)
    extra_product(1)
    add_down(*group_rows(extra_places))
    extra_sum(1)

    def rest(group, carry):
        add_down(*group_rows(group_places(group)))
        return carry

    lax.fori_loop((GROUPS - CATCH_UP) * CATCH_EACH, CATCH_UP, rest, 0)

    def moved_down(slot, carry):
        trial = keeper_ref[slot]
        new_down_ref[slot] = down_v[trial] - rate_ref[trial] * (down_sum[trial] * INV_WIDTH)
        return carry

    lax.fori_loop(0, TRIALS, moved_down, 0)

    def last(group, carry):
        finish(group)
        return carry

    lax.fori_loop(GROUPS - FINISH_LAG, GROUPS + 1, last, 0)

    for step in range(COUNT):
        every(step, lambda *what: sending(*what).wait_send())
    for kind in (0, 1):
        swap(kind, 0).wait_send()
    for kind in (0, 1):
        z_copy(kind, 0).wait_send()
    for name in SMALL:
        if not name.startswith("hid_x"):
            sends[name]().wait_send()

    @pl.when(x == row)
    def _():
        for name in trio("hid_x"):
            sends[name]().wait_send()

    def drain(number, carry):
        core_copy(number).wait_send()
        return carry

    def drain_far(number, carry):
        far_copy(number).wait_send()
        return carry

    lax.fori_loop(0, SENT, drain, 0)
    lax.fori_loop(0, 16, drain_far, 0)


def write_out(*refs):
    sources, targets, sems = refs[:3], refs[3:6], refs[6]
    copies = [pltpu.make_async_copy(sources[at], targets[at], sems.at[at]) for at in range(3)]
    for copy in copies:
        copy.start()
    for copy in copies:
        copy.wait()


def per_device(
    packed_input_rows,
    frozen_weight,
    down_adapters,
    up_adapters,
    trial_learning_rates,
    row_trial_index,
    output_gradient,
    keeper_slot,
):
    width_in, width_out = frozen_weight.shape
    all_rows = row_trial_index.shape[0]
    block_rows = output_gradient.shape[0]
    vmem = pl.BlockSpec(memory_space=pltpu.VMEM)
    smem = pl.BlockSpec(memory_space=pltpu.SMEM)
    hbm = pl.BlockSpec(memory_space=pl.ANY)
    dma = pltpu.SemaphoreType.DMA
    f32, bf16 = jnp.float32, jnp.bfloat16
    half = TRIALS // 2
    held = pl.pallas_call(
        whole_kernel,
        name="adapter_sweep",
        out_shape=(
            pltpu.VMEM((block_rows, width_out), bf16),
            pltpu.VMEM(down_adapters.shape, f32),
            pltpu.VMEM(up_adapters.shape, f32),
        ),
        in_specs=[hbm, hbm, hbm, hbm, smem, vmem, hbm, smem],
        out_specs=(vmem, vmem, vmem),
        scratch_shapes=[
            pltpu.VMEM((all_rows, width_in), bf16),
            pltpu.VMEM((width_in, width_out), bf16),
            pltpu.VMEM((4 * PIECE, width_out), f32),
            pltpu.VMEM((2 * PIECE, width_out), f32),
            pltpu.VMEM((SENT, PIECE, width_out), bf16),
            pltpu.VMEM((SENT, PIECE, width_out), bf16),
            pltpu.VMEM((block_rows, width_out), f32),
            pltpu.VMEM((block_rows, width_out), bf16),
            pltpu.VMEM((block_rows, width_out), bf16),
            pltpu.VMEM(down_adapters.shape, f32),
            pltpu.VMEM((FLAT, width_in), bf16),
            pltpu.VMEM(up_adapters.shape, f32),
            pltpu.VMEM((FLAT, width_out), bf16),
            pltpu.VMEM((block_rows, width_out), bf16),
            pltpu.VMEM(down_adapters.shape, f32),
            pltpu.VMEM((all_rows, FLAT), bf16),
            pltpu.VMEM((block_rows, FLAT), bf16),
            pltpu.VMEM((RANK, SHARD), f32),
            pltpu.VMEM((RANK, SHARD), f32),
            pltpu.VMEM((RANK, SHARD), f32),
            pltpu.VMEM((RANK, SHARD), f32),
            pltpu.VMEM((32, RANK, SHARD), bf16),
            pltpu.VMEM((4, RANK, 256), f32),
            pltpu.VMEM((4, RANK, 256), f32),
            pltpu.VMEM((4, RANK, 256), f32),
            pltpu.VMEM((4, RANK, 256), f32),
            pltpu.VMEM((4, RANK, 256), f32),
            pltpu.VMEM((16, RANK, 256), bf16),
            pltpu.VMEM((TRIALS, RANK, width_out), f32),
            pltpu.VMEM((half, RANK, width_out), f32),
            pltpu.VMEM((half, RANK, width_out), bf16),
            pltpu.VMEM((half, RANK, width_out), bf16),
            pltpu.VMEM((TRIALS, RANK, width_out), f32),
            dma((5,)),
            dma((2, 2, len(ITEMS))),
            dma((2, 2, len(ITEMS))),
            dma((2,)),
            dma((2,)),
            dma((2,)),
            dma((2,)),
            dma((SENT,)),
            dma((SENT,)),
            dma((16,)),
            dma((16,)),
            dma((len(SMALL),)),
            dma((len(SMALL),)),
        ],
        compiler_params=pltpu.CompilerParams(
            collective_id=0, has_side_effects=True, vmem_limit_bytes=56 << 20
        ),
        cost_estimate=pl.CostEstimate(flops=22 * 10**9, bytes_accessed=20 << 20, transcendentals=0),
    )(
        packed_input_rows, frozen_weight, down_adapters, up_adapters, trial_learning_rates,
        row_trial_index.reshape(32, all_rows // 32), output_gradient, keeper_slot,
    )
    held = [pltpu.with_memory_space_constraint(array, pltpu.VMEM) for array in held]
    return tuple(pl.pallas_call(
        write_out,
        name="write_out",
        out_shape=tuple(jax.ShapeDtypeStruct(array.shape, array.dtype) for array in held),
        in_specs=[vmem] * len(held),
        out_specs=tuple([hbm] * len(held)),
        scratch_shapes=[dma((len(held),))],
        compiler_params=pltpu.CompilerParams(vmem_limit_bytes=1 << 20),
    )(*held))


def solution(mesh):
    in_specs = (
        P("col", "row"),
        P("row", "col"),
        P(None, None, "row"),
        P(None, None, "col"),
        P(),
        P(),
        P("row", "col"),
        P(),
    )
    out_specs = (P("row", "col"), P(None, None, "row"), P(None, None, "col"))
    return jax.shard_map(
        per_device, mesh=mesh, in_specs=in_specs, out_specs=out_specs, check_vma=False
    )
```

```python
import jax
import jax.numpy as jnp
from jax import lax
from jax.experimental import pallas as pl
from jax.experimental.pallas import tpu as pltpu
from jax.sharding import PartitionSpec as P

MESH = pl.DeviceIdType.MESH
D = 8192
RANK = 16
TRIALS = 16
FLAT = RANK * TRIALS
SHARD = 128
PIECE = 64
HALF = 32
SCALE = 2.0 / RANK
INV_WIDTH = D ** (-0.5)

STEPS = (
    (
        (("F", 0),),
        (("L", 0, 0),),
        (("L", 1, 0),),
        (("RF", 0), ("RL", 0, 0)),
        (("L", 3, 0),),
        (("L", 0, 1),),
        (("L", 2, 0),),
        (("F", 1),),
        (("RL", 1, 0), ("RL", 3, 0)),
        (("L", 2, 1),),
        (("L", 3, 1),),
        (("RL", 0, 1), ("RL", 2, 0)),
        (("L", 1, 1),),
        (("RL", 2, 1), ("RL", 3, 1)),
        (("RL", 1, 1),),
    ),
    (
        (("F", 0),),
        (("L", 0, 0),),
        (("L", 1, 0),),
        (("RF", 0), ("RL", 0, 0)),
        (("L", 3, 0),),
        (("L", 0, 1),),
        (("L", 2, 0),),
        (("F", 1),),
        (("RL", 1, 0), ("RL", 3, 0)),
        (("L", 2, 1),),
        (("L", 1, 1),),
        (("RL", 2, 0), ("RL", 2, 1)),
        (("L", 3, 1),),
        (("RL", 0, 1), ("RL", 1, 1)),
        (("RL", 3, 1),),
    ),
)
ITEMS = tuple(item for step in STEPS[0] for item in step)
COUNT = len(STEPS[0])
SWAP_SENT, SWAP_USED = 2, 5
Z_GROUP = 3
GROUPS = COUNT
TURN = [step + (step >= Z_GROUP) for step in range(COUNT)]


def offsets(kind, first, last, zz):
    return (first, last, zz, 0) if kind == 0 else (last, first, zz, 1)


def landed(axis, item):
    name, zz = item[0], item[-1]
    kind = axis if name in ("F", "RF") else 1 - axis
    if name == "F":
        return [offsets(kind, 3, 0, zz), offsets(kind, 2 if zz else 1, 0, zz)]
    if name == "RF":
        return [offsets(kind, 2, 0, zz)]
    if name == "L":
        return [offsets(kind, item[1], 3, zz), offsets(kind, item[1], 1, zz)]
    return [offsets(kind, item[1], 2, zz)]


def group_pieces():
    groups = []
    for step in range(COUNT):
        groups.append([
            piece for axis in (0, 1) for item in STEPS[axis][step] for piece in landed(axis, item)
        ])
    groups.insert(Z_GROUP, [(0, 0, 0, 0), (0, 0, 1, 0), (0, 0, 0, 1), (0, 0, 1, 1)])
    groups[-1] = [offsets(kind, 1, 0, 1) for kind in (0, 1)] + groups[-1]
    return groups


CODES = [[dx + 4 * dy + 16 * dz + 32 * kind for dx, dy, dz, kind in group] for group in group_pieces()]


def piece_slots():
    seen, slots = [0, 0], []
    for group in group_pieces():
        slots.append([])
        for piece in group:
            odd = piece[0] % 2
            slots[-1].append(seen[odd])
            seen[odd] += 1
    return slots


SLOTS = piece_slots()
SENT = 32
SMALL = (
    ["hid_core", "hid_far", "hid_z"] + [f"hid_y{k}" for k in (1, 2, 3)] + [f"hid_x{k}" for k in (1, 2, 3)]
    + [f"grad_x{k}" for k in (1, 2, 3)] + [f"grad_y{k}" for k in (1, 2, 3)] + ["grad_z"]
    + [f"low_x{k}" for k in (1, 2, 3)] + ["low_core", "low_far", "up_core", "up_far", "up_share"]
)
FINISH, FINISH_EACH, FINISHED = 11, 3, 9
CATCH_UP, CATCH_EACH = 10, 3


def select(index, values):
    out = jnp.int32(values[0])
    for at in range(1, len(values)):
        out = jnp.where(index == at, jnp.int32(values[at]), out)
    return out


def whole_kernel(
    x_ref, w_ref, down_ref, up_ref, rate_ref, trial_ref, grad_ref, keeper_ref,
    proj_ref, new_down_ref, new_up_ref,
    xg, w_v, keep, keep_half, stage, recv_core, total, z_stage, recv_z,
    down_v, down_low, up_v, up_low, grad_v, down_sum, grad_wide, hid_wide,
    hid_part, hid_core, hid_half, hid_far, hid_low,
    grad_part, grad_sum, grad_x, grad_y, grad_z, grad_low,
    up_part, up_core, up_half, up_far, up_sum,
    local_sem, send_sem, recv_sem, z_send, z_recv, swap_send, swap_recv, core_send, core_recv, far_send, far_recv,
    small_send, small_recv,
):
    row = lax.axis_index("row")
    col = lax.axis_index("col")
    z_hi, core = row // 2, row % 2
    x, y, z_lo = col // 8, (col // 2) % 4, col % 2
    contract_last = (((1,), (1,)), ((), ()))
    contract_first = (((0,), (0,)), ((), ()))

    def base(piece):
        dx, dy, dz, kind = piece
        return ((x + dx) % 4 * 8 + (y + dy) % 4 * 2 + (z_lo + dz) % 2) * SHARD + kind * PIECE

    def neighbour(axis, way):
        if axis == 0:
            return (row, (x + way) % 4 * 8 + y * 2 + z_lo)
        return (row, x * 8 + (y + way) % 4 * 2 + z_lo)

    z_mate = (row, x * 8 + y * 2 + 1 - z_lo)
    core_mate = (z_hi * 2 + 1 - core, col)
    far_mate = ((1 - z_hi) * 2 + core, col)

    loads = [
        pltpu.make_async_copy(source, target, local_sem.at[at])
        for at, (source, target) in enumerate((
            (x_ref, xg.at[pl.ds(pl.multiple_of(col * SHARD, SHARD), SHARD)]),
            (down_ref, down_v), (up_ref, up_v), (grad_ref, grad_v), (w_ref, w_v),
        ))
    ]
    for load in loads:
        load.start()
    own, down_load, up_load, grad_load, weight_load = loads

    barrier = pltpu.get_barrier_semaphore()
    mates = [neighbour(axis, way) for axis in (0, 1) for way in (1, 2, 3)] + [z_mate, core_mate, far_mate]
    for mate in mates:
        pl.semaphore_signal(barrier, inc=1, device_id=mate, device_id_type=MESH)
    pl.semaphore_wait(barrier, len(mates))
    own.wait()

    def remote(start, rows, ssem, rsem, mate):
        spot = xg.at[pl.ds(pl.multiple_of(start, HALF), rows)]
        return pltpu.make_async_remote_copy(
            src_ref=spot, dst_ref=spot, send_sem=ssem, recv_sem=rsem, device_id=mate, device_id_type=MESH
        )

    def sending(axis, way, item):
        name, zz = item[0], item[-1]
        kind = axis if name in ("F", "RF") else 1 - axis
        back = 3 if way == 0 else 1
        if name == "F":
            start, rows = base(offsets(kind, way if zz else 0, 0, zz)), PIECE
        elif name == "RF":
            start, rows = base(offsets(kind, back, 0, zz)) + way * HALF, HALF
        elif name == "L":
            start, rows = base(offsets(kind, item[1], 0, zz)), PIECE
        else:
            start, rows = base(offsets(kind, item[1], back, zz)) + way * HALF, HALF
        at = ITEMS.index(item)
        return remote(
            start, rows, send_sem.at[axis, way, at], recv_sem.at[axis, way, at],
            neighbour(axis, 1 if way == 0 else 3),
        )

    def receiving(axis, way, item):
        pieces = landed(axis, item)
        if len(pieces) == 2:
            start, rows = base(pieces[way]), PIECE
        else:
            start, rows = base(pieces[0]) + way * HALF, HALF
        at = ITEMS.index(item)
        return remote(
            start, rows, send_sem.at[axis, way, at], recv_sem.at[axis, way, at],
            neighbour(axis, 1 if way == 0 else 3),
        )

    def every(step, action):
        for axis in (0, 1):
            for item in STEPS[axis][step]:
                for way in (0, 1):
                    action(axis, way, item)

    def send(step):
        every(step, lambda *what: sending(*what).start())

    def sent(step):
        every(step, lambda *what: sending(*what).wait_send())

    def arrive(step):
        every(step, lambda *what: receiving(*what).wait_recv())

    def z_copy(kind, dz):
        return remote(base((0, 0, dz, kind)), PIECE, z_send.at[kind], z_recv.at[kind], z_mate)

    def swap(kind, dz):
        return remote(base(offsets(kind, 1, 0, dz)), PIECE, swap_send.at[kind], swap_recv.at[kind], z_mate)

    send(0)
    for kind in (0, 1):
        z_copy(kind, 0).start()
    send(1)

    def small(name, source, target, mate):
        at = SMALL.index(name)
        return pltpu.make_async_remote_copy(
            src_ref=source, dst_ref=target, send_sem=small_send.at[at], recv_sem=small_recv.at[at],
            device_id=mate, device_id_type=MESH,
        )

    own_slot = y * 2 + z_lo
    half = pl.ds(core * (TRIALS // 2), TRIALS // 2)
    other_half = pl.ds((1 - core) * (TRIALS // 2), TRIALS // 2)
    sends = {
        "hid_core": lambda: small("hid_core", hid_part, hid_core, core_mate),
        "hid_far": lambda: small("hid_far", hid_half, hid_far, far_mate),
        "hid_z": lambda: small("hid_z", hid_low.at[own_slot], hid_low.at[own_slot], z_mate),
        "grad_z": lambda: small("grad_z", grad_part, grad_z, z_mate),
        "low_core": lambda: small(
            "low_core", grad_low.at[pl.ds(row * 4, 4)], grad_low.at[pl.ds(row * 4, 4)], core_mate),
        "low_far": lambda: small(
            "low_far", grad_low.at[pl.ds(z_hi * 8, 8)], grad_low.at[pl.ds(z_hi * 8, 8)], far_mate),
        "up_core": lambda: small("up_core", up_part.at[other_half], up_core, core_mate),
        "up_far": lambda: small("up_far", up_half, up_far, far_mate),
        "up_share": lambda: small("up_share", up_sum.at[half], up_sum.at[half], core_mate),
    }
    for way in (1, 2, 3):
        def along(way=way):
            to_x, to_y = neighbour(0, way), neighbour(1, way)
            block = pl.ds(y * 2, 2)
            sends[f"hid_y{way}"] = lambda: small(f"hid_y{way}", hid_low.at[block], hid_low.at[block], to_y)
            sends[f"hid_x{way}"] = lambda: small(
                f"hid_x{way}", hid_low.at[own_slot], hid_low.at[own_slot], to_x)
            sends[f"grad_x{way}"] = lambda: small(
                f"grad_x{way}", grad_sum.at[(x + way) % 4], grad_x.at[x], to_x)
            sends[f"grad_y{way}"] = lambda: small(f"grad_y{way}", grad_y.at[y], grad_y.at[y], to_y)
            own_chunk = row * 4 + x
            sends[f"low_x{way}"] = lambda: small(
                f"low_x{way}", grad_low.at[own_chunk], grad_low.at[own_chunk], to_x)
        along()

    def go(*names):
        for name in names:
            sends[name]().start()

    def come(*names):
        for name in names:
            sends[name]().wait_recv()

    def trio(name):
        return [f"{name}{way}" for way in (1, 2, 3)]

    def bounds(shape, axis):
        label = lax.broadcasted_iota(jnp.int32, shape, axis) // RANK
        low, high = jnp.zeros(shape, jnp.int32), jnp.zeros(shape, jnp.int32)
        first = jnp.zeros((1, 1), jnp.int32)
        for trial in range(TRIALS):
            count = jnp.sum((trial_ref[...] <= trial).astype(jnp.int32), keepdims=True)
            low = jnp.where(label == trial, first, low)
            high = jnp.where(label == trial, count, high)
            first = count
        return low, high

    lane_low, lane_high = bounds((1, FLAT), 1)
    side_low, side_high = bounds((FLAT, 1), 0)
    spread = (
        lax.broadcasted_iota(jnp.int32, (RANK, FLAT), 1) % RANK
        == lax.broadcasted_iota(jnp.int32, (RANK, FLAT), 0)
    ).astype(jnp.bfloat16)

    def pick_rank(full, start):
        rows = full.shape[1]
        where = start + lax.broadcasted_iota(jnp.int32, (FLAT, rows), 1)
        mine = jnp.where((where >= side_low) & (where < side_high), full, 0.0)
        return jnp.sum(mine.reshape(TRIALS, RANK, rows), axis=0)

    def widen(low, start):
        values = lax.dot_general(low, spread, contract_first, preferred_element_type=jnp.float32)
        where = start + lax.broadcasted_iota(jnp.int32, values.shape, 0)
        return jnp.where((where >= lane_low) & (where < lane_high), values, 0.0).astype(jnp.bfloat16)

    down_load.wait()

    def cast_down(trial, carry):
        down_low[pl.ds(pl.multiple_of(trial * RANK, RANK), RANK), :] = down_v[trial].astype(jnp.bfloat16)
        return carry

    lax.fori_loop(0, TRIALS, cast_down, 0)
    own_rows = xg[pl.ds(pl.multiple_of(col * SHARD, SHARD), SHARD), :]
    hid_part[...] = pick_rank(
        lax.dot_general(down_low[...], own_rows, contract_last, preferred_element_type=jnp.float32), col * SHARD
    )
    go("hid_core")

    down_sum[...] = jnp.zeros_like(down_sum)
    total[...] = jnp.zeros_like(total)
    weight_load.wait()

    def hid_0():
        come("hid_core")
        hid_half[...] = hid_part[...] + hid_core[...]
        go("hid_far")

    def hid_1():
        come("hid_far")

        @pl.when(x == row)
        def _():
            hid_low[own_slot] = ((hid_half[...] + hid_far[...]) * INV_WIDTH).astype(jnp.bfloat16)
            go(*trio("hid_x"))

    def hid_2():
        for way in (1, 2, 3):
            @pl.when((x - way + 4) % 4 == row)
            def _():
                sends[f"hid_x{way}"]().wait_recv()

        go("hid_z")

    def hid_3():
        come("hid_z")
        go(*trio("hid_y"))

    def hid_4():
        come(*trio("hid_y"))

    def grad_0():
        up_load.wait()
        for trial in range(TRIALS):
            up_low[trial * RANK:(trial + 1) * RANK, :] = up_v[trial].astype(jnp.bfloat16)
        grad_load.wait()

        def gradient_chunk(chunk, carry):
            start = pl.multiple_of(chunk * 256, 256)
            full = lax.dot_general(
                up_low[...], grad_v[pl.ds(start, 256), :], contract_last, preferred_element_type=jnp.float32
            )
            grad_part[chunk] = pick_rank(full, row * 8 * SHARD + start)
            return carry

        lax.fori_loop(0, 4, gradient_chunk, 0)

    def grad_1():
        come("grad_z")
        grad_sum[...] = grad_part[...] + grad_z[...]
        go(*trio("grad_x"))
        grad_x[x] = grad_sum[x]

    def grad_2():
        come(*trio("grad_x"))
        grad_y[y] = (grad_x[0] + grad_x[1]) + (grad_x[2] + grad_x[3])
        go(*trio("grad_y"))

    def grad_3():
        come(*trio("grad_y"))
        gradient = (grad_y[0] + grad_y[1]) + (grad_y[2] + grad_y[3])
        grad_low[row * 4 + x] = (gradient * SCALE).astype(jnp.bfloat16)
        go(*trio("low_x"))

    def grad_4():
        come(*trio("low_x"))
        go("low_core")

    def grad_5():
        come("low_core")
        go("low_far")

    def widen_gradient(side):
        def wide(number, carry):
            chunk = side * 8 + number
            start = pl.multiple_of(chunk * 256, 256)
            grad_wide[pl.ds(start, 256), :] = widen(grad_low[chunk], start)
            return carry

        lax.fori_loop(0, 8, wide, 0)

    def grad_6():
        widen_gradient(z_hi)

    def grad_7():
        come("low_far")
        widen_gradient(1 - z_hi)

    def up_0():
        def wide(block, carry):
            start = pl.multiple_of(block * SHARD, SHARD)
            hid_wide[pl.ds(start, SHARD), :] = widen(hid_low[block], row * 8 * SHARD + start)
            return carry

        lax.fori_loop(0, 8, wide, 0)
        full = lax.dot_general(hid_wide[...], grad_v[...], contract_first, preferred_element_type=jnp.float32)
        up_part[...] = full.reshape(up_part.shape)
        go("up_core")

    def up_1():
        come("up_core")
        up_half[...] = (up_part[half] + up_core[...]).astype(jnp.bfloat16)
        go("up_far")

    def up_2():
        come("up_far")
        up_sum[half] = up_half[...].astype(jnp.float32) + up_far[...].astype(jnp.float32)
        go("up_share")

    def up_3():
        come("up_share")

        def moved(slot, carry):
            trial = keeper_ref[slot]
            new_up_ref[slot] = up_v[trial] - rate_ref[trial] * (up_sum[trial] * SCALE)
            return carry

        lax.fori_loop(0, TRIALS, moved, 0)

    def adapter_term():
        def adapter(block, carry):
            spot = pl.ds(pl.multiple_of(block * SHARD, SHARD), SHARD)
            total[spot, :] += SCALE * jnp.dot(
                hid_wide[spot, :], up_low[...], preferred_element_type=jnp.float32
            )
            return carry

        lax.fori_loop(0, 8, adapter, 0)

    ahead = {0: [hid_0], 2: [hid_1, grad_1], 4: [hid_2, grad_2], 6: [hid_3, grad_3], 8: [hid_4, grad_4],
             9: [grad_5], 10: [up_1], 12: [up_2]}
    after = {7: [], 8: [up_0], 9: [grad_6, adapter_term], 10: [grad_7], 13: [up_3]}
    grad_0()
    go("grad_z")

    def decode(code):
        dx, dy, dz, kind = code % 4, code // 4 % 4, code // 16 % 2, code // 32
        return (x + dx) % 4, base((dx, dy, dz, kind))

    def core_copy(slot):
        return pltpu.make_async_remote_copy(
            src_ref=stage.at[slot], dst_ref=recv_core.at[slot],
            send_sem=core_send.at[slot], recv_sem=core_recv.at[slot],
            device_id=core_mate, device_id_type=MESH,
        )

    def far_copy(number):
        spot = pl.ds(pl.multiple_of(number * PIECE, PIECE), PIECE)
        return pltpu.make_async_remote_copy(
            src_ref=z_stage.at[spot], dst_ref=recv_z.at[spot],
            send_sem=far_send.at[number], recv_sem=far_recv.at[number],
            device_id=far_mate, device_id_type=MESH,
        )

    def group_places(group):
        return [decode(select(group, [codes[slot] for codes in CODES])) for slot in range(4)]

    def group_rows(places):
        starts = [pl.multiple_of(start, PIECE) for _, start in places]
        return starts, jnp.concatenate([xg[pl.ds(start, PIECE), :] for start in starts], axis=0)

    def add_down(starts, rows):
        wide = jnp.concatenate([grad_wide[pl.ds(start, PIECE), :] for start in starts], axis=0)
        down_sum[...] += lax.dot_general(
            wide, rows, contract_first, preferred_element_type=jnp.float32
        ).reshape(down_sum.shape)

    def finish(group):
        places = group_places(group)
        for slot in range(4):
            plane, start = places[slot]

            @pl.when(plane == row)
            def _():
                number = start % (8 * SHARD) // PIECE
                far_copy(number).wait_recv()
                spot = pl.ds(pl.multiple_of(number * PIECE, PIECE), PIECE)
                proj_ref[spot, :] = (total[spot, :] + recv_z[spot, :].astype(jnp.float32)).astype(jnp.bfloat16)

    def add_core(place, own_sum, slot):
        plane, start = place
        number = start % (8 * SHARD) // PIECE
        spot = pl.ds(pl.multiple_of(number * PIECE, PIECE), PIECE)
        summed = own_sum + recv_core[slot].astype(jnp.float32)

        @pl.when(plane // 2 == z_hi)
        def _():
            total[spot, :] += summed

        @pl.when(plane // 2 != z_hi)
        def _():
            z_stage[spot, :] = summed.astype(jnp.bfloat16)
            far_copy(number).start()

    def hand_over(places, slots, product):
        for at, (plane, _) in enumerate(places):
            @pl.when(plane % 2 != core)
            def _():
                stage[slots[at]] = product[at * PIECE:(at + 1) * PIECE].astype(jnp.bfloat16)
                core_copy(slots[at]).start()

    def take_over(places, slots, own_sums):
        for at, place in enumerate(places):
            @pl.when(place[0] % 2 == core)
            def _():
                core_copy(slots[at]).wait_recv()
                add_core(place, own_sums[at * PIECE:(at + 1) * PIECE, :], slots[at])

    extra_places = group_places(GROUPS)

    def extra_product(part):
        places, slots = extra_places[2 * part:2 * part + 2], SLOTS[GROUPS][2 * part:2 * part + 2]
        _, rows = group_rows(places)
        product = jnp.dot(rows, w_v[...], preferred_element_type=jnp.float32)
        keep_half[...] = product
        hand_over(places, slots, product)

    def extra_sum(part):
        take_over(extra_places[2 * part:2 * part + 2], SLOTS[GROUPS][2 * part:2 * part + 2], keep_half)

    after[7].append(lambda: extra_product(0))
    after[8].insert(0, lambda: extra_sum(0))

    def body(group, carry):
        @pl.when(group == Z_GROUP)
        def _():
            for work in ahead.get(Z_GROUP, ()):
                work()

        for step in range(COUNT - 1):
            @pl.when(group == TURN[step])
            def _():
                arrive(step)
                if step == Z_GROUP - 1:
                    for kind in (0, 1):
                        z_copy(kind, 1).wait_recv()
                if step == SWAP_USED:
                    for kind in (0, 1):
                        swap(kind, 1).wait_recv()
                if step + 2 < COUNT:
                    send(step + 2)
                for work in ahead.get(TURN[step], ()):
                    work()
                if step >= 2:
                    sent(step - 2)
                if step == SWAP_SENT:
                    for kind in (0, 1):
                        swap(kind, 0).start()

        places = group_places(group)
        starts, rows = group_rows(places)
        product = jnp.dot(rows, w_v[...], preferred_element_type=jnp.float32)
        keep[...] = product
        slots = [select(group, [each[at] for each in SLOTS]) for at in range(4)]
        hand_over(places, slots, product)

        for at, works in after.items():
            @pl.when(group == at)
            def _():
                for work in works:
                    work()

        @pl.when(group >= CATCH_UP)
        def _():
            add_down(*group_rows(group_places(group)))

        take_over(places, slots, keep)

        @pl.when(group >= CATCH_UP)
        def _():
            def earlier(number, carry):
                before = (group - CATCH_UP - 1) * CATCH_EACH + 1 + number

                @pl.when((before >= 0) & (before < CATCH_UP))
                def _():
                    add_down(*group_rows(group_places(before)))

                return carry

            lax.fori_loop(0, CATCH_EACH, earlier, 0)

        @pl.when((group >= FINISH) & (group < FINISH + FINISHED // FINISH_EACH))
        def _():
            for number in range(FINISH_EACH):
                finish((group - FINISH) * FINISH_EACH + number)

        return carry

    lax.fori_loop(0, GROUPS, body, 0)

    arrive(COUNT - 1)
    extra_product(1)
    add_down(*group_rows(extra_places))
    extra_sum(1)

    def moved_down(slot, carry):
        trial = keeper_ref[slot]
        new_down_ref[slot] = down_v[trial] - rate_ref[trial] * (down_sum[trial] * INV_WIDTH)
        return carry

    lax.fori_loop(0, TRIALS, moved_down, 0)

    def last(group, carry):
        finish(group)
        return carry

    lax.fori_loop(FINISHED, GROUPS, last, 0)

    for step in range(COUNT - 3, COUNT):
        sent(step)
    for kind in (0, 1):
        swap(kind, 0).wait_send()
    for kind in (0, 1):
        z_copy(kind, 0).wait_send()
    for name in SMALL:
        if not name.startswith("hid_x"):
            sends[name]().wait_send()

    @pl.when(x == row)
    def _():
        for name in trio("hid_x"):
            sends[name]().wait_send()

    def drain(number, carry):
        core_copy(number).wait_send()
        return carry

    lax.fori_loop(0, SENT, drain, 0)
    finish(GROUPS)

    def drain_far(number, carry):
        far_copy(number).wait_send()
        return carry

    lax.fori_loop(0, 16, drain_far, 0)


def write_out(*refs):
    sources, targets, sems = refs[:3], refs[3:6], refs[6]
    copies = [pltpu.make_async_copy(sources[at], targets[at], sems.at[at]) for at in range(3)]
    for copy in copies:
        copy.start()
    for copy in copies:
        copy.wait()


def per_device(
    packed_input_rows,
    frozen_weight,
    down_adapters,
    up_adapters,
    trial_learning_rates,
    row_trial_index,
    output_gradient,
    keeper_slot,
):
    width_in, width_out = frozen_weight.shape
    all_rows = row_trial_index.shape[0]
    block_rows = output_gradient.shape[0]
    vmem = pl.BlockSpec(memory_space=pltpu.VMEM)
    smem = pl.BlockSpec(memory_space=pltpu.SMEM)
    hbm = pl.BlockSpec(memory_space=pl.ANY)
    dma = pltpu.SemaphoreType.DMA
    f32, bf16 = jnp.float32, jnp.bfloat16
    half = TRIALS // 2
    held = pl.pallas_call(
        whole_kernel,
        name="adapter_sweep",
        out_shape=(
            pltpu.VMEM((block_rows, width_out), bf16),
            pltpu.VMEM(down_adapters.shape, f32),
            pltpu.VMEM(up_adapters.shape, f32),
        ),
        in_specs=[hbm, hbm, hbm, hbm, smem, vmem, hbm, smem],
        out_specs=(vmem, vmem, vmem),
        scratch_shapes=[
            pltpu.VMEM((all_rows, width_in), bf16),
            pltpu.VMEM((width_in, width_out), bf16),
            pltpu.VMEM((4 * PIECE, width_out), f32),
            pltpu.VMEM((2 * PIECE, width_out), f32),
            pltpu.VMEM((SENT, PIECE, width_out), bf16),
            pltpu.VMEM((SENT, PIECE, width_out), bf16),
            pltpu.VMEM((block_rows, width_out), f32),
            pltpu.VMEM((block_rows, width_out), bf16),
            pltpu.VMEM((block_rows, width_out), bf16),
            pltpu.VMEM(down_adapters.shape, f32),
            pltpu.VMEM((FLAT, width_in), bf16),
            pltpu.VMEM(up_adapters.shape, f32),
            pltpu.VMEM((FLAT, width_out), bf16),
            pltpu.VMEM((block_rows, width_out), bf16),
            pltpu.VMEM(down_adapters.shape, f32),
            pltpu.VMEM((all_rows, FLAT), bf16),
            pltpu.VMEM((block_rows, FLAT), bf16),
            pltpu.VMEM((RANK, SHARD), f32),
            pltpu.VMEM((RANK, SHARD), f32),
            pltpu.VMEM((RANK, SHARD), f32),
            pltpu.VMEM((RANK, SHARD), f32),
            pltpu.VMEM((8, RANK, SHARD), bf16),
            pltpu.VMEM((4, RANK, 256), f32),
            pltpu.VMEM((4, RANK, 256), f32),
            pltpu.VMEM((4, RANK, 256), f32),
            pltpu.VMEM((4, RANK, 256), f32),
            pltpu.VMEM((4, RANK, 256), f32),
            pltpu.VMEM((16, RANK, 256), bf16),
            pltpu.VMEM((TRIALS, RANK, width_out), f32),
            pltpu.VMEM((half, RANK, width_out), f32),
            pltpu.VMEM((half, RANK, width_out), bf16),
            pltpu.VMEM((half, RANK, width_out), bf16),
            pltpu.VMEM((TRIALS, RANK, width_out), f32),
            dma((5,)),
            dma((2, 2, len(ITEMS))),
            dma((2, 2, len(ITEMS))),
            dma((2,)),
            dma((2,)),
            dma((2,)),
            dma((2,)),
            dma((SENT,)),
            dma((SENT,)),
            dma((16,)),
            dma((16,)),
            dma((len(SMALL),)),
            dma((len(SMALL),)),
        ],
        compiler_params=pltpu.CompilerParams(
            collective_id=0, has_side_effects=True, vmem_limit_bytes=56 << 20
        ),
        cost_estimate=pl.CostEstimate(flops=22 * 10**9, bytes_accessed=20 << 20, transcendentals=0),
    )(
        packed_input_rows, frozen_weight, down_adapters, up_adapters, trial_learning_rates,
        row_trial_index.reshape(32, all_rows // 32), output_gradient, keeper_slot,
    )
    held = [pltpu.with_memory_space_constraint(array, pltpu.VMEM) for array in held]
    return tuple(pl.pallas_call(
        write_out,
        name="write_out",
        out_shape=tuple(jax.ShapeDtypeStruct(array.shape, array.dtype) for array in held),
        in_specs=[vmem] * len(held),
        out_specs=tuple([hbm] * len(held)),
        scratch_shapes=[dma((len(held),))],
        compiler_params=pltpu.CompilerParams(vmem_limit_bytes=1 << 20),
    )(*held))


def solution(mesh):
    in_specs = (
        P("col", "row"),
        P("row", "col"),
        P(None, None, "row"),
        P(None, None, "col"),
        P(),
        P(),
        P("row", "col"),
        P(),
    )
    out_specs = (P("row", "col"), P(None, None, "row"), P(None, None, "col"))
    return jax.shard_map(
        per_device, mesh=mesh, in_specs=in_specs, out_specs=out_specs, check_vma=False
    )
```

```python
import jax
import jax.numpy as jnp
from jax import lax
from jax.experimental import pallas as pl
from jax.experimental.pallas import tpu as pltpu
from jax.sharding import PartitionSpec as P

MESH = pl.DeviceIdType.MESH
D = 8192
RANK = 16
TRIALS = 16
FLAT = RANK * TRIALS
SHARD = 128
PIECE = 64
HALF = 32
SCALE = 2.0 / RANK
INV_WIDTH = D ** (-0.5)

STEPS = (
    (
        (("F", 0),),
        (("L", 0, 0),),
        (("L", 1, 0),),
        (("RF", 0), ("RL", 0, 0)),
        (("L", 3, 0),),
        (("L", 0, 1),),
        (("L", 2, 0),),
        (("F", 1),),
        (("RL", 1, 0), ("RL", 3, 0)),
        (("L", 2, 1),),
        (("L", 3, 1),),
        (("RL", 0, 1), ("RL", 2, 0)),
        (("L", 1, 1),),
        (("RL", 2, 1), ("RL", 3, 1)),
        (("RL", 1, 1),),
    ),
    (
        (("F", 0),),
        (("L", 0, 0),),
        (("L", 1, 0),),
        (("RF", 0), ("RL", 0, 0)),
        (("L", 3, 0),),
        (("L", 0, 1),),
        (("L", 2, 0),),
        (("F", 1),),
        (("RL", 1, 0), ("RL", 3, 0)),
        (("L", 2, 1),),
        (("L", 1, 1),),
        (("RL", 2, 0), ("RL", 2, 1)),
        (("L", 3, 1),),
        (("RL", 0, 1), ("RL", 1, 1)),
        (("RL", 3, 1),),
    ),
)
ITEMS = tuple(item for step in STEPS[0] for item in step)
COUNT = len(STEPS[0])
SWAP_SENT, SWAP_USED = 2, 5
Z_GROUP = 3
GROUPS = COUNT
TURN = [step + (step >= Z_GROUP) for step in range(COUNT)]


def step_of(axis, item):
    return [item in step for step in STEPS[axis]].index(True)


def needed(axis, item):
    name, zz = item[0], item[-1]
    if name in ("RF", "RL"):
        return step_of(axis, ("F" if name == "RF" else "L",) + item[1:])
    if name == "F" or item[1] == 0:
        return SWAP_USED if (name, zz) == ("F", 1) else Z_GROUP - 1 if zz else -1
    if zz:
        return SWAP_USED if item[1] == 1 else step_of(1 - axis, ("F", 1))
    return step_of(1 - axis, ("RF" if item[1] == 2 else "F", 0))


def offsets(kind, first, last, zz):
    return (first, last, zz, 0) if kind == 0 else (last, first, zz, 1)


def landed(axis, item):
    name, zz = item[0], item[-1]
    kind = axis if name in ("F", "RF") else 1 - axis
    if name == "F":
        return [offsets(kind, 3, 0, zz), offsets(kind, 2 if zz else 1, 0, zz)]
    if name == "RF":
        return [offsets(kind, 2, 0, zz)]
    if name == "L":
        return [offsets(kind, item[1], 3, zz), offsets(kind, item[1], 1, zz)]
    return [offsets(kind, item[1], 2, zz)]


def group_pieces():
    groups = []
    for step in range(COUNT):
        groups.append([
            piece for axis in (0, 1) for item in STEPS[axis][step] for piece in landed(axis, item)
        ])
    groups.insert(Z_GROUP, [(0, 0, 0, 0), (0, 0, 1, 0), (0, 0, 0, 1), (0, 0, 1, 1)])
    groups[-1] = [offsets(kind, 1, 0, 1) for kind in (0, 1)] + groups[-1]
    return groups


CODES = [[dx + 4 * dy + 16 * dz + 32 * kind for dx, dy, dz, kind in group] for group in group_pieces()]


def piece_slots():
    seen, slots = [0, 0], []
    for group in group_pieces():
        slots.append([])
        for piece in group:
            odd = piece[0] % 2
            slots[-1].append(seen[odd])
            seen[odd] += 1
    return slots


SLOTS = piece_slots()
SENT = 32
SMALL = (
    ["hid_core", "hid_far", "hid_z"] + [f"hid_y{k}" for k in (1, 2, 3)] + [f"hid_x{k}" for k in (1, 2, 3)]
    + [f"grad_x{k}" for k in (1, 2, 3)] + [f"grad_y{k}" for k in (1, 2, 3)] + ["grad_z"]
    + [f"low_x{k}" for k in (1, 2, 3)] + ["low_core", "low_far", "up_core", "up_far", "up_share"]
)
FINISH, FINISH_EACH, FINISHED = 11, 3, 9
CATCH_UP, CATCH_EACH = 10, 2


def select(index, values):
    out = jnp.int32(values[0])
    for at in range(1, len(values)):
        out = jnp.where(index == at, jnp.int32(values[at]), out)
    return out


def whole_kernel(
    x_ref, w_ref, down_ref, up_ref, rate_ref, trial_ref, grad_ref, keeper_ref,
    proj_ref, new_down_ref, new_up_ref,
    xg, w_v, keep, keep_half, stage, recv_core, total, z_stage, recv_z,
    down_v, down_low, up_v, up_low, grad_v, down_sum, grad_wide, hid_wide,
    hid_part, hid_core, hid_half, hid_far, hid_low,
    grad_part, grad_sum, grad_x, grad_y, grad_z, grad_low,
    up_part, up_core, up_half, up_far, up_sum,
    local_sem, send_sem, recv_sem, z_send, z_recv, swap_send, swap_recv, core_send, core_recv, far_send, far_recv,
    small_send, small_recv,
):
    row = lax.axis_index("row")
    col = lax.axis_index("col")
    z_hi, core = row // 2, row % 2
    x, y, z_lo = col // 8, (col // 2) % 4, col % 2
    contract_last = (((1,), (1,)), ((), ()))
    contract_first = (((0,), (0,)), ((), ()))

    def base(piece):
        dx, dy, dz, kind = piece
        return ((x + dx) % 4 * 8 + (y + dy) % 4 * 2 + (z_lo + dz) % 2) * SHARD + kind * PIECE

    def neighbour(axis, way):
        if axis == 0:
            return (row, (x + way) % 4 * 8 + y * 2 + z_lo)
        return (row, x * 8 + (y + way) % 4 * 2 + z_lo)

    z_mate = (row, x * 8 + y * 2 + 1 - z_lo)
    core_mate = (z_hi * 2 + 1 - core, col)
    far_mate = ((1 - z_hi) * 2 + core, col)

    loads = [
        pltpu.make_async_copy(source, target, local_sem.at[at])
        for at, (source, target) in enumerate((
            (x_ref, xg.at[pl.ds(pl.multiple_of(col * SHARD, SHARD), SHARD)]),
            (down_ref, down_v), (up_ref, up_v), (grad_ref, grad_v), (w_ref, w_v),
        ))
    ]
    for load in loads:
        load.start()
    own, down_load, up_load, grad_load, weight_load = loads

    barrier = pltpu.get_barrier_semaphore()
    mates = [neighbour(axis, way) for axis in (0, 1) for way in (1, 2, 3)] + [z_mate, core_mate, far_mate]
    for mate in mates:
        pl.semaphore_signal(barrier, inc=1, device_id=mate, device_id_type=MESH)
    pl.semaphore_wait(barrier, len(mates))
    own.wait()

    def remote(start, rows, ssem, rsem, mate):
        spot = xg.at[pl.ds(pl.multiple_of(start, HALF), rows)]
        return pltpu.make_async_remote_copy(
            src_ref=spot, dst_ref=spot, send_sem=ssem, recv_sem=rsem, device_id=mate, device_id_type=MESH
        )

    def sending(axis, way, item):
        name, zz = item[0], item[-1]
        kind = axis if name in ("F", "RF") else 1 - axis
        back = 3 if way == 0 else 1
        if name == "F":
            start, rows = base(offsets(kind, way if zz else 0, 0, zz)), PIECE
        elif name == "RF":
            start, rows = base(offsets(kind, back, 0, zz)) + way * HALF, HALF
        elif name == "L":
            start, rows = base(offsets(kind, item[1], 0, zz)), PIECE
        else:
            start, rows = base(offsets(kind, item[1], back, zz)) + way * HALF, HALF
        at = ITEMS.index(item)
        return remote(
            start, rows, send_sem.at[axis, way, at], recv_sem.at[axis, way, at],
            neighbour(axis, 1 if way == 0 else 3),
        )

    def receiving(axis, way, item):
        pieces = landed(axis, item)
        if len(pieces) == 2:
            start, rows = base(pieces[way]), PIECE
        else:
            start, rows = base(pieces[0]) + way * HALF, HALF
        at = ITEMS.index(item)
        return remote(
            start, rows, send_sem.at[axis, way, at], recv_sem.at[axis, way, at],
            neighbour(axis, 1 if way == 0 else 3),
        )

    def every(step, action):
        for axis in (0, 1):
            for item in STEPS[axis][step]:
                for way in (0, 1):
                    action(axis, way, item)

    def send(step, early=None):
        def start(axis, way, item):
            if early is None or early == (needed(axis, item) < step - 2):
                sending(axis, way, item).start()

        every(step, start)

    def sent(step):
        every(step, lambda *what: sending(*what).wait_send())

    def arrive(step):
        every(step, lambda *what: receiving(*what).wait_recv())

    def z_copy(kind, dz):
        return remote(base((0, 0, dz, kind)), PIECE, z_send.at[kind], z_recv.at[kind], z_mate)

    def swap(kind, dz):
        return remote(base(offsets(kind, 1, 0, dz)), PIECE, swap_send.at[kind], swap_recv.at[kind], z_mate)

    send(0)
    for kind in (0, 1):
        z_copy(kind, 0).start()
    send(1)

    def small(name, source, target, mate):
        at = SMALL.index(name)
        return pltpu.make_async_remote_copy(
            src_ref=source, dst_ref=target, send_sem=small_send.at[at], recv_sem=small_recv.at[at],
            device_id=mate, device_id_type=MESH,
        )

    own_slot = y * 2 + z_lo
    half = pl.ds(core * (TRIALS // 2), TRIALS // 2)
    other_half = pl.ds((1 - core) * (TRIALS // 2), TRIALS // 2)
    sends = {
        "hid_core": lambda: small("hid_core", hid_part, hid_core, core_mate),
        "hid_far": lambda: small("hid_far", hid_half, hid_far, far_mate),
        "hid_z": lambda: small("hid_z", hid_low.at[own_slot], hid_low.at[own_slot], z_mate),
        "grad_z": lambda: small("grad_z", grad_part, grad_z, z_mate),
        "low_core": lambda: small(
            "low_core", grad_low.at[pl.ds(row * 4, 4)], grad_low.at[pl.ds(row * 4, 4)], core_mate),
        "low_far": lambda: small(
            "low_far", grad_low.at[pl.ds(z_hi * 8, 8)], grad_low.at[pl.ds(z_hi * 8, 8)], far_mate),
        "up_core": lambda: small("up_core", up_part.at[other_half], up_core, core_mate),
        "up_far": lambda: small("up_far", up_half, up_far, far_mate),
        "up_share": lambda: small("up_share", up_sum.at[half], up_sum.at[half], core_mate),
    }
    for way in (1, 2, 3):
        def along(way=way):
            to_x, to_y = neighbour(0, way), neighbour(1, way)
            block = pl.ds(y * 2, 2)
            sends[f"hid_y{way}"] = lambda: small(f"hid_y{way}", hid_low.at[block], hid_low.at[block], to_y)
            sends[f"hid_x{way}"] = lambda: small(
                f"hid_x{way}", hid_low.at[own_slot], hid_low.at[own_slot], to_x)
            sends[f"grad_x{way}"] = lambda: small(
                f"grad_x{way}", grad_sum.at[(x + way) % 4], grad_x.at[x], to_x)
            sends[f"grad_y{way}"] = lambda: small(f"grad_y{way}", grad_y.at[y], grad_y.at[y], to_y)
            own_chunk = row * 4 + x
            sends[f"low_x{way}"] = lambda: small(
                f"low_x{way}", grad_low.at[own_chunk], grad_low.at[own_chunk], to_x)
        along()

    def go(*names):
        for name in names:
            sends[name]().start()

    def come(*names):
        for name in names:
            sends[name]().wait_recv()

    def trio(name):
        return [f"{name}{way}" for way in (1, 2, 3)]

    def bounds(shape, axis):
        label = lax.broadcasted_iota(jnp.int32, shape, axis) // RANK
        low, high = jnp.zeros(shape, jnp.int32), jnp.zeros(shape, jnp.int32)
        first = jnp.zeros((1, 1), jnp.int32)
        for trial in range(TRIALS):
            count = jnp.sum((trial_ref[...] <= trial).astype(jnp.int32), keepdims=True)
            low = jnp.where(label == trial, first, low)
            high = jnp.where(label == trial, count, high)
            first = count
        return low, high

    lane_low, lane_high = bounds((1, FLAT), 1)
    side_low, side_high = bounds((FLAT, 1), 0)
    spread = (
        lax.broadcasted_iota(jnp.int32, (RANK, FLAT), 1) % RANK
        == lax.broadcasted_iota(jnp.int32, (RANK, FLAT), 0)
    ).astype(jnp.bfloat16)

    def pick_rank(full, start):
        rows = full.shape[1]
        where = start + lax.broadcasted_iota(jnp.int32, (FLAT, rows), 1)
        mine = jnp.where((where >= side_low) & (where < side_high), full, 0.0)
        return jnp.sum(mine.reshape(TRIALS, RANK, rows), axis=0)

    def widen(low, start):
        values = lax.dot_general(low, spread, contract_first, preferred_element_type=jnp.float32)
        where = start + lax.broadcasted_iota(jnp.int32, values.shape, 0)
        return jnp.where((where >= lane_low) & (where < lane_high), values, 0.0).astype(jnp.bfloat16)

    down_load.wait()

    def cast_down(trial, carry):
        down_low[pl.ds(pl.multiple_of(trial * RANK, RANK), RANK), :] = down_v[trial].astype(jnp.bfloat16)
        return carry

    lax.fori_loop(0, TRIALS, cast_down, 0)
    own_rows = xg[pl.ds(pl.multiple_of(col * SHARD, SHARD), SHARD), :]
    hid_part[...] = pick_rank(
        lax.dot_general(down_low[...], own_rows, contract_last, preferred_element_type=jnp.float32), col * SHARD
    )
    go("hid_core")

    down_sum[...] = jnp.zeros_like(down_sum)
    total[...] = jnp.zeros_like(total)
    weight_load.wait()

    def hid_0():
        come("hid_core")
        hid_half[...] = hid_part[...] + hid_core[...]
        go("hid_far")

    def hid_1():
        come("hid_far")

        @pl.when(x == row)
        def _():
            hid_low[own_slot] = ((hid_half[...] + hid_far[...]) * INV_WIDTH).astype(jnp.bfloat16)
            go(*trio("hid_x"))

    def hid_2():
        for way in (1, 2, 3):
            @pl.when((x - way + 4) % 4 == row)
            def _():
                sends[f"hid_x{way}"]().wait_recv()

        go("hid_z")

    def hid_3():
        come("hid_z")
        go(*trio("hid_y"))

    def hid_4():
        come(*trio("hid_y"))

    def grad_0():
        up_load.wait()
        for trial in range(TRIALS):
            up_low[trial * RANK:(trial + 1) * RANK, :] = up_v[trial].astype(jnp.bfloat16)
        grad_load.wait()

        def gradient_chunk(chunk, carry):
            start = pl.multiple_of(chunk * 256, 256)
            full = lax.dot_general(
                up_low[...], grad_v[pl.ds(start, 256), :], contract_last, preferred_element_type=jnp.float32
            )
            grad_part[chunk] = pick_rank(full, row * 8 * SHARD + start)
            return carry

        lax.fori_loop(0, 4, gradient_chunk, 0)

    def grad_1():
        come("grad_z")
        grad_sum[...] = grad_part[...] + grad_z[...]
        go(*trio("grad_x"))
        grad_x[x] = grad_sum[x]

    def grad_2():
        come(*trio("grad_x"))
        grad_y[y] = (grad_x[0] + grad_x[1]) + (grad_x[2] + grad_x[3])
        go(*trio("grad_y"))

    def grad_3():
        come(*trio("grad_y"))
        gradient = (grad_y[0] + grad_y[1]) + (grad_y[2] + grad_y[3])
        grad_low[row * 4 + x] = (gradient * SCALE).astype(jnp.bfloat16)
        go(*trio("low_x"))

    def grad_4():
        come(*trio("low_x"))
        go("low_core")

    def grad_5():
        come("low_core")
        go("low_far")

    def widen_gradient(side):
        def wide(number, carry):
            chunk = side * 8 + number
            start = pl.multiple_of(chunk * 256, 256)
            grad_wide[pl.ds(start, 256), :] = widen(grad_low[chunk], start)
            return carry

        lax.fori_loop(0, 8, wide, 0)

    def grad_6():
        widen_gradient(z_hi)

    def grad_7():
        come("low_far")
        widen_gradient(1 - z_hi)

    def up_0():
        def wide(block, carry):
            start = pl.multiple_of(block * SHARD, SHARD)
            hid_wide[pl.ds(start, SHARD), :] = widen(hid_low[block], row * 8 * SHARD + start)
            return carry

        lax.fori_loop(0, 8, wide, 0)
        full = lax.dot_general(hid_wide[...], grad_v[...], contract_first, preferred_element_type=jnp.float32)
        up_part[...] = full.reshape(up_part.shape)
        go("up_core")

    def up_1():
        come("up_core")
        up_half[...] = (up_part[half] + up_core[...]).astype(jnp.bfloat16)
        go("up_far")

    def up_2():
        come("up_far")
        up_sum[half] = up_half[...].astype(jnp.float32) + up_far[...].astype(jnp.float32)
        go("up_share")

    def up_3():
        come("up_share")

        def moved(slot, carry):
            trial = keeper_ref[slot]
            new_up_ref[slot] = up_v[trial] - rate_ref[trial] * (up_sum[trial] * SCALE)
            return carry

        lax.fori_loop(0, TRIALS, moved, 0)

    def adapter_term():
        def adapter(block, carry):
            spot = pl.ds(pl.multiple_of(block * SHARD, SHARD), SHARD)
            total[spot, :] += SCALE * jnp.dot(
                hid_wide[spot, :], up_low[...], preferred_element_type=jnp.float32
            )
            return carry

        lax.fori_loop(0, 8, adapter, 0)

    ahead = {0: [hid_0], 2: [hid_1, grad_1], 4: [hid_2, grad_2], 6: [hid_3, grad_3], 8: [hid_4, grad_4],
             9: [grad_5], 10: [up_1], 12: [up_2]}
    after = {7: [], 8: [up_0], 9: [grad_6, adapter_term], 10: [grad_7], 13: [up_3]}
    grad_0()
    go("grad_z")

    def decode(code):
        dx, dy, dz, kind = code % 4, code // 4 % 4, code // 16 % 2, code // 32
        return (x + dx) % 4, base((dx, dy, dz, kind))

    def core_copy(slot):
        return pltpu.make_async_remote_copy(
            src_ref=stage.at[slot], dst_ref=recv_core.at[slot],
            send_sem=core_send.at[slot], recv_sem=core_recv.at[slot],
            device_id=core_mate, device_id_type=MESH,
        )

    def far_copy(number):
        spot = pl.ds(pl.multiple_of(number * PIECE, PIECE), PIECE)
        return pltpu.make_async_remote_copy(
            src_ref=z_stage.at[spot], dst_ref=recv_z.at[spot],
            send_sem=far_send.at[number], recv_sem=far_recv.at[number],
            device_id=far_mate, device_id_type=MESH,
        )

    def group_places(group):
        return [decode(select(group, [codes[slot] for codes in CODES])) for slot in range(4)]

    def group_rows(places):
        starts = [pl.multiple_of(start, PIECE) for _, start in places]
        return starts, jnp.concatenate([xg[pl.ds(start, PIECE), :] for start in starts], axis=0)

    def add_down(starts, rows):
        wide = jnp.concatenate([grad_wide[pl.ds(start, PIECE), :] for start in starts], axis=0)
        down_sum[...] += lax.dot_general(
            wide, rows, contract_first, preferred_element_type=jnp.float32
        ).reshape(down_sum.shape)

    def finish(group):
        places = group_places(group)
        for slot in range(4):
            plane, start = places[slot]

            @pl.when(plane == row)
            def _():
                number = start % (8 * SHARD) // PIECE
                far_copy(number).wait_recv()
                spot = pl.ds(pl.multiple_of(number * PIECE, PIECE), PIECE)
                proj_ref[spot, :] = (total[spot, :] + recv_z[spot, :].astype(jnp.float32)).astype(jnp.bfloat16)

    def add_core(place, own_sum, slot):
        plane, start = place
        number = start % (8 * SHARD) // PIECE
        spot = pl.ds(pl.multiple_of(number * PIECE, PIECE), PIECE)
        summed = own_sum + recv_core[slot].astype(jnp.float32)

        @pl.when(plane // 2 == z_hi)
        def _():
            total[spot, :] += summed

        @pl.when(plane // 2 != z_hi)
        def _():
            z_stage[spot, :] = summed.astype(jnp.bfloat16)
            far_copy(number).start()

    def hand_over(places, slots, product):
        for at, (plane, _) in enumerate(places):
            @pl.when(plane % 2 != core)
            def _():
                stage[slots[at]] = product[at * PIECE:(at + 1) * PIECE].astype(jnp.bfloat16)
                core_copy(slots[at]).start()

    def take_over(places, slots, own_sums):
        for at, place in enumerate(places):
            @pl.when(place[0] % 2 == core)
            def _():
                core_copy(slots[at]).wait_recv()
                add_core(place, own_sums[at * PIECE:(at + 1) * PIECE, :], slots[at])

    extra_places = group_places(GROUPS)

    def extra_product(part):
        places, slots = extra_places[2 * part:2 * part + 2], SLOTS[GROUPS][2 * part:2 * part + 2]
        _, rows = group_rows(places)
        product = jnp.dot(rows, w_v[...], preferred_element_type=jnp.float32)
        keep_half[...] = product
        hand_over(places, slots, product)

    def extra_sum(part):
        take_over(extra_places[2 * part:2 * part + 2], SLOTS[GROUPS][2 * part:2 * part + 2], keep_half)

    after[7].append(lambda: extra_product(0))
    after[8].insert(0, lambda: extra_sum(0))

    def body(group, carry):
        @pl.when(group == Z_GROUP)
        def _():
            for work in ahead.get(Z_GROUP, ()):
                work()

        for step in range(COUNT - 1):
            @pl.when(group == TURN[step])
            def _():
                if step + 2 < COUNT:
                    send(step + 2, early=True)
                arrive(step)
                if step == Z_GROUP - 1:
                    for kind in (0, 1):
                        z_copy(kind, 1).wait_recv()
                if step == SWAP_USED:
                    for kind in (0, 1):
                        swap(kind, 1).wait_recv()
                if step + 2 < COUNT:
                    send(step + 2, early=False)
                for work in ahead.get(TURN[step], ()):
                    work()
                if step >= 2:
                    sent(step - 2)
                if step == SWAP_SENT:
                    for kind in (0, 1):
                        swap(kind, 0).start()

        places = group_places(group)
        starts, rows = group_rows(places)
        product = jnp.dot(rows, w_v[...], preferred_element_type=jnp.float32)
        keep[...] = product
        slots = [select(group, [each[at] for each in SLOTS]) for at in range(4)]
        hand_over(places, slots, product)

        for at, works in after.items():
            @pl.when(group == at)
            def _():
                for work in works:
                    work()

        @pl.when(group >= CATCH_UP)
        def _():
            add_down(*group_rows(group_places(group)))

        take_over(places, slots, keep)

        @pl.when(group >= CATCH_UP)
        def _():
            def earlier(number, carry):
                before = (group - CATCH_UP - 1) * CATCH_EACH + 1 + number

                @pl.when((before >= 0) & (before < 7))
                def _():
                    add_down(*group_rows(group_places(before)))

                return carry

            lax.fori_loop(0, CATCH_EACH, earlier, 0)

        @pl.when((group >= FINISH) & (group < FINISH + FINISHED // FINISH_EACH))
        def _():
            for number in range(FINISH_EACH):
                finish((group - FINISH) * FINISH_EACH + number)

        return carry

    lax.fori_loop(0, GROUPS, body, 0)

    arrive(COUNT - 1)
    extra_product(1)
    add_down(*group_rows(extra_places))
    extra_sum(1)

    def rest(group, carry):
        add_down(*group_rows(group_places(group)))
        return carry

    lax.fori_loop(7, CATCH_UP, rest, 0)

    def moved_down(slot, carry):
        trial = keeper_ref[slot]
        new_down_ref[slot] = down_v[trial] - rate_ref[trial] * (down_sum[trial] * INV_WIDTH)
        return carry

    lax.fori_loop(0, TRIALS, moved_down, 0)

    def last(group, carry):
        finish(group)
        return carry

    lax.fori_loop(FINISHED, GROUPS, last, 0)

    for step in range(COUNT - 3, COUNT):
        sent(step)
    for kind in (0, 1):
        swap(kind, 0).wait_send()
    for kind in (0, 1):
        z_copy(kind, 0).wait_send()
    for name in SMALL:
        if not name.startswith("hid_x"):
            sends[name]().wait_send()

    @pl.when(x == row)
    def _():
        for name in trio("hid_x"):
            sends[name]().wait_send()

    def drain(number, carry):
        core_copy(number).wait_send()
        return carry

    lax.fori_loop(0, SENT, drain, 0)
    finish(GROUPS)

    def drain_far(number, carry):
        far_copy(number).wait_send()
        return carry

    lax.fori_loop(0, 16, drain_far, 0)


def write_out(*refs):
    sources, targets, sems = refs[:3], refs[3:6], refs[6]
    copies = [pltpu.make_async_copy(sources[at], targets[at], sems.at[at]) for at in range(3)]
    for copy in copies:
        copy.start()
    for copy in copies:
        copy.wait()


def per_device(
    packed_input_rows,
    frozen_weight,
    down_adapters,
    up_adapters,
    trial_learning_rates,
    row_trial_index,
    output_gradient,
    keeper_slot,
):
    width_in, width_out = frozen_weight.shape
    all_rows = row_trial_index.shape[0]
    block_rows = output_gradient.shape[0]
    vmem = pl.BlockSpec(memory_space=pltpu.VMEM)
    smem = pl.BlockSpec(memory_space=pltpu.SMEM)
    hbm = pl.BlockSpec(memory_space=pl.ANY)
    dma = pltpu.SemaphoreType.DMA
    f32, bf16 = jnp.float32, jnp.bfloat16
    half = TRIALS // 2
    held = pl.pallas_call(
        whole_kernel,
        name="adapter_sweep",
        out_shape=(
            pltpu.VMEM((block_rows, width_out), bf16),
            pltpu.VMEM(down_adapters.shape, f32),
            pltpu.VMEM(up_adapters.shape, f32),
        ),
        in_specs=[hbm, hbm, hbm, hbm, smem, vmem, hbm, smem],
        out_specs=(vmem, vmem, vmem),
        scratch_shapes=[
            pltpu.VMEM((all_rows, width_in), bf16),
            pltpu.VMEM((width_in, width_out), bf16),
            pltpu.VMEM((4 * PIECE, width_out), f32),
            pltpu.VMEM((2 * PIECE, width_out), f32),
            pltpu.VMEM((SENT, PIECE, width_out), bf16),
            pltpu.VMEM((SENT, PIECE, width_out), bf16),
            pltpu.VMEM((block_rows, width_out), f32),
            pltpu.VMEM((block_rows, width_out), bf16),
            pltpu.VMEM((block_rows, width_out), bf16),
            pltpu.VMEM(down_adapters.shape, f32),
            pltpu.VMEM((FLAT, width_in), bf16),
            pltpu.VMEM(up_adapters.shape, f32),
            pltpu.VMEM((FLAT, width_out), bf16),
            pltpu.VMEM((block_rows, width_out), bf16),
            pltpu.VMEM(down_adapters.shape, f32),
            pltpu.VMEM((all_rows, FLAT), bf16),
            pltpu.VMEM((block_rows, FLAT), bf16),
            pltpu.VMEM((RANK, SHARD), f32),
            pltpu.VMEM((RANK, SHARD), f32),
            pltpu.VMEM((RANK, SHARD), f32),
            pltpu.VMEM((RANK, SHARD), f32),
            pltpu.VMEM((8, RANK, SHARD), bf16),
            pltpu.VMEM((4, RANK, 256), f32),
            pltpu.VMEM((4, RANK, 256), f32),
            pltpu.VMEM((4, RANK, 256), f32),
            pltpu.VMEM((4, RANK, 256), f32),
            pltpu.VMEM((4, RANK, 256), f32),
            pltpu.VMEM((16, RANK, 256), bf16),
            pltpu.VMEM((TRIALS, RANK, width_out), f32),
            pltpu.VMEM((half, RANK, width_out), f32),
            pltpu.VMEM((half, RANK, width_out), bf16),
            pltpu.VMEM((half, RANK, width_out), bf16),
            pltpu.VMEM((TRIALS, RANK, width_out), f32),
            dma((5,)),
            dma((2, 2, len(ITEMS))),
            dma((2, 2, len(ITEMS))),
            dma((2,)),
            dma((2,)),
            dma((2,)),
            dma((2,)),
            dma((SENT,)),
            dma((SENT,)),
            dma((16,)),
            dma((16,)),
            dma((len(SMALL),)),
            dma((len(SMALL),)),
        ],
        compiler_params=pltpu.CompilerParams(
            collective_id=0, has_side_effects=True, vmem_limit_bytes=56 << 20
        ),
        cost_estimate=pl.CostEstimate(flops=22 * 10**9, bytes_accessed=20 << 20, transcendentals=0),
    )(
        packed_input_rows, frozen_weight, down_adapters, up_adapters, trial_learning_rates,
        row_trial_index.reshape(32, all_rows // 32), output_gradient, keeper_slot,
    )
    held = [pltpu.with_memory_space_constraint(array, pltpu.VMEM) for array in held]
    return tuple(pl.pallas_call(
        write_out,
        name="write_out",
        out_shape=tuple(jax.ShapeDtypeStruct(array.shape, array.dtype) for array in held),
        in_specs=[vmem] * len(held),
        out_specs=tuple([hbm] * len(held)),
        scratch_shapes=[dma((len(held),))],
        compiler_params=pltpu.CompilerParams(vmem_limit_bytes=1 << 20),
    )(*held))


def solution(mesh):
    in_specs = (
        P("col", "row"),
        P("row", "col"),
        P(None, None, "row"),
        P(None, None, "col"),
        P(),
        P(),
        P("row", "col"),
        P(),
    )
    out_specs = (P("row", "col"), P(None, None, "row"), P(None, None, "col"))
    return jax.shard_map(
        per_device, mesh=mesh, in_specs=in_specs, out_specs=out_specs, check_vma=False
    )
```

```python
import jax
import jax.numpy as jnp
from jax import lax
from jax.experimental import pallas as pl
from jax.experimental.pallas import tpu as pltpu
from jax.sharding import PartitionSpec as P

MESH = pl.DeviceIdType.MESH
D = 8192
RANK = 16
TRIALS = 16
FLAT = RANK * TRIALS
SHARD = 128
PIECE = 64
HALF = 32
SCALE = 2.0 / RANK
INV_WIDTH = D ** (-0.5)

STEPS = (
    (
        (("F", 0),),
        (("L", 0, 0),),
        (("L", 1, 0),),
        (("RF", 0), ("RL", 0, 0)),
        (("L", 3, 0),),
        (("L", 0, 1),),
        (("L", 2, 0),),
        (("F", 1),),
        (("RL", 1, 0), ("RL", 3, 0)),
        (("L", 2, 1),),
        (("L", 3, 1),),
        (("RL", 0, 1), ("RL", 2, 0)),
        (("L", 1, 1),),
        (("RL", 2, 1), ("RL", 3, 1)),
        (("RL", 1, 1),),
    ),
    (
        (("F", 0),),
        (("L", 0, 0),),
        (("L", 1, 0),),
        (("RF", 0), ("RL", 0, 0)),
        (("L", 3, 0),),
        (("L", 0, 1),),
        (("L", 2, 0),),
        (("F", 1),),
        (("RL", 1, 0), ("RL", 3, 0)),
        (("L", 2, 1),),
        (("L", 1, 1),),
        (("RL", 2, 0), ("RL", 2, 1)),
        (("L", 3, 1),),
        (("RL", 0, 1), ("RL", 1, 1)),
        (("RL", 3, 1),),
    ),
)
ITEMS = tuple(item for step in STEPS[0] for item in step)
COUNT = len(STEPS[0])
SWAP_SENT, SWAP_USED = 2, 5
Z_GROUP = 3
GROUPS = COUNT
TURN = [step + (step >= Z_GROUP) for step in range(COUNT)]


def offsets(kind, first, last, zz):
    return (first, last, zz, 0) if kind == 0 else (last, first, zz, 1)


def landed(axis, item):
    name, zz = item[0], item[-1]
    kind = axis if name in ("F", "RF") else 1 - axis
    if name == "F":
        return [offsets(kind, 3, 0, zz), offsets(kind, 2 if zz else 1, 0, zz)]
    if name == "RF":
        return [offsets(kind, 2, 0, zz)]
    if name == "L":
        return [offsets(kind, item[1], 3, zz), offsets(kind, item[1], 1, zz)]
    return [offsets(kind, item[1], 2, zz)]


def group_pieces():
    groups = []
    for step in range(COUNT):
        groups.append([
            piece for axis in (0, 1) for item in STEPS[axis][step] for piece in landed(axis, item)
        ])
    groups.insert(Z_GROUP, [(0, 0, 0, 0), (0, 0, 1, 0), (0, 0, 0, 1), (0, 0, 1, 1)])
    groups[-1] = [offsets(kind, 1, 0, 1) for kind in (0, 1)] + groups[-1]
    return groups


CODES = [[dx + 4 * dy + 16 * dz + 32 * kind for dx, dy, dz, kind in group] for group in group_pieces()]


def piece_slots():
    seen, slots = [0, 0], []
    for group in group_pieces():
        slots.append([])
        for piece in group:
            odd = piece[0] % 2
            slots[-1].append(seen[odd])
            seen[odd] += 1
    return slots


SLOTS = piece_slots()
SENT = 32
SMALL = (
    ["hid_core", "hid_far", "hid_z"] + [f"hid_y{k}" for k in (1, 2, 3)] + [f"hid_x{k}" for k in (1, 2, 3)]
    + [f"grad_x{k}" for k in (1, 2, 3)] + [f"grad_y{k}" for k in (1, 2, 3)] + ["grad_z"]
    + [f"low_x{k}" for k in (1, 2, 3)] + ["low_core", "low_far", "up_core", "up_far", "up_share"]
)
FINISH, FINISH_EACH, FINISHED = 11, 3, 9
CATCH_UP, CATCH_EACH = 10, 3


def select(index, values):
    out = jnp.int32(values[0])
    for at in range(1, len(values)):
        out = jnp.where(index == at, jnp.int32(values[at]), out)
    return out


def whole_kernel(
    x_ref, w_ref, down_ref, up_ref, rate_ref, trial_ref, grad_ref, keeper_ref,
    proj_ref, new_down_ref, new_up_ref,
    xg, w_v, keep, keep_half, stage, recv_core, total, z_stage, recv_z,
    down_v, down_low, up_v, up_low, grad_v, down_sum, grad_wide, hid_wide,
    hid_part, hid_core, hid_half, hid_far, hid_low,
    grad_part, grad_sum, grad_x, grad_y, grad_z, grad_low,
    up_part, up_core, up_half, up_far, up_sum,
    local_sem, send_sem, recv_sem, z_send, z_recv, swap_send, swap_recv, core_send, core_recv, far_send, far_recv,
    small_send, small_recv,
):
    row = lax.axis_index("row")
    col = lax.axis_index("col")
    z_hi, core = row // 2, row % 2
    x, y, z_lo = col // 8, (col // 2) % 4, col % 2
    contract_last = (((1,), (1,)), ((), ()))
    contract_first = (((0,), (0,)), ((), ()))

    def base(piece):
        dx, dy, dz, kind = piece
        return ((x + dx) % 4 * 8 + (y + dy) % 4 * 2 + (z_lo + dz) % 2) * SHARD + kind * PIECE

    def neighbour(axis, way):
        if axis == 0:
            return (row, (x + way) % 4 * 8 + y * 2 + z_lo)
        return (row, x * 8 + (y + way) % 4 * 2 + z_lo)

    z_mate = (row, x * 8 + y * 2 + 1 - z_lo)
    core_mate = (z_hi * 2 + 1 - core, col)
    far_mate = ((1 - z_hi) * 2 + core, col)

    loads = [
        pltpu.make_async_copy(source, target, local_sem.at[at])
        for at, (source, target) in enumerate((
            (x_ref, xg.at[pl.ds(pl.multiple_of(col * SHARD, SHARD), SHARD)]),
            (down_ref, down_v), (up_ref, up_v), (grad_ref, grad_v), (w_ref, w_v),
        ))
    ]
    for load in loads:
        load.start()
    own, down_load, up_load, grad_load, weight_load = loads

    barrier = pltpu.get_barrier_semaphore()
    mates = [neighbour(axis, way) for axis in (0, 1) for way in (1, 2, 3)] + [z_mate, core_mate, far_mate]
    for mate in mates:
        pl.semaphore_signal(barrier, inc=1, device_id=mate, device_id_type=MESH)
    pl.semaphore_wait(barrier, len(mates))
    own.wait()

    def remote(start, rows, ssem, rsem, mate):
        spot = xg.at[pl.ds(pl.multiple_of(start, HALF), rows)]
        return pltpu.make_async_remote_copy(
            src_ref=spot, dst_ref=spot, send_sem=ssem, recv_sem=rsem, device_id=mate, device_id_type=MESH
        )

    def sending(axis, way, item):
        name, zz = item[0], item[-1]
        kind = axis if name in ("F", "RF") else 1 - axis
        back = 3 if way == 0 else 1
        if name == "F":
            start, rows = base(offsets(kind, way if zz else 0, 0, zz)), PIECE
        elif name == "RF":
            start, rows = base(offsets(kind, back, 0, zz)) + way * HALF, HALF
        elif name == "L":
            start, rows = base(offsets(kind, item[1], 0, zz)), PIECE
        else:
            start, rows = base(offsets(kind, item[1], back, zz)) + way * HALF, HALF
        at = ITEMS.index(item)
        return remote(
            start, rows, send_sem.at[axis, way, at], recv_sem.at[axis, way, at],
            neighbour(axis, 1 if way == 0 else 3),
        )

    def receiving(axis, way, item):
        pieces = landed(axis, item)
        if len(pieces) == 2:
            start, rows = base(pieces[way]), PIECE
        else:
            start, rows = base(pieces[0]) + way * HALF, HALF
        at = ITEMS.index(item)
        return remote(
            start, rows, send_sem.at[axis, way, at], recv_sem.at[axis, way, at],
            neighbour(axis, 1 if way == 0 else 3),
        )

    def every(step, action):
        for axis in (0, 1):
            for item in STEPS[axis][step]:
                for way in (0, 1):
                    action(axis, way, item)

    def send(step):
        every(step, lambda *what: sending(*what).start())

    def sent(step):
        every(step, lambda *what: sending(*what).wait_send())

    def arrive(step):
        every(step, lambda *what: receiving(*what).wait_recv())

    def z_copy(kind, dz):
        return remote(base((0, 0, dz, kind)), PIECE, z_send.at[kind], z_recv.at[kind], z_mate)

    def swap(kind, dz):
        return remote(base(offsets(kind, 1, 0, dz)), PIECE, swap_send.at[kind], swap_recv.at[kind], z_mate)

    send(0)
    for kind in (0, 1):
        z_copy(kind, 0).start()
    send(1)

    def small(name, source, target, mate):
        at = SMALL.index(name)
        return pltpu.make_async_remote_copy(
            src_ref=source, dst_ref=target, send_sem=small_send.at[at], recv_sem=small_recv.at[at],
            device_id=mate, device_id_type=MESH,
        )

    own_slot = y * 2 + z_lo
    half = pl.ds(core * (TRIALS // 2), TRIALS // 2)
    other_half = pl.ds((1 - core) * (TRIALS // 2), TRIALS // 2)
    sends = {
        "hid_core": lambda: small("hid_core", hid_part, hid_core, core_mate),
        "hid_far": lambda: small("hid_far", hid_half, hid_far, far_mate),
        "hid_z": lambda: small("hid_z", hid_low.at[own_slot], hid_low.at[own_slot], z_mate),
        "grad_z": lambda: small("grad_z", grad_part, grad_z, z_mate),
        "low_core": lambda: small(
            "low_core", grad_low.at[pl.ds(row * 4, 4)], grad_low.at[pl.ds(row * 4, 4)], core_mate),
        "low_far": lambda: small(
            "low_far", grad_low.at[pl.ds(z_hi * 8, 8)], grad_low.at[pl.ds(z_hi * 8, 8)], far_mate),
        "up_core": lambda: small("up_core", up_part.at[other_half], up_core, core_mate),
        "up_far": lambda: small("up_far", up_half, up_far, far_mate),
        "up_share": lambda: small("up_share", up_sum.at[half], up_sum.at[half], core_mate),
    }
    for way in (1, 2, 3):
        def along(way=way):
            to_x, to_y = neighbour(0, way), neighbour(1, way)
            block = pl.ds(y * 2, 2)
            sends[f"hid_y{way}"] = lambda: small(f"hid_y{way}", hid_low.at[block], hid_low.at[block], to_y)
            sends[f"hid_x{way}"] = lambda: small(
                f"hid_x{way}", hid_low.at[own_slot], hid_low.at[own_slot], to_x)
            sends[f"grad_x{way}"] = lambda: small(
                f"grad_x{way}", grad_sum.at[(x + way) % 4], grad_x.at[x], to_x)
            sends[f"grad_y{way}"] = lambda: small(f"grad_y{way}", grad_y.at[y], grad_y.at[y], to_y)
            own_chunk = row * 4 + x
            sends[f"low_x{way}"] = lambda: small(
                f"low_x{way}", grad_low.at[own_chunk], grad_low.at[own_chunk], to_x)
        along()

    def go(*names):
        for name in names:
            sends[name]().start()

    def come(*names):
        for name in names:
            sends[name]().wait_recv()

    def trio(name):
        return [f"{name}{way}" for way in (1, 2, 3)]

    def bounds(shape, axis):
        label = lax.broadcasted_iota(jnp.int32, shape, axis) // RANK
        low, high = jnp.zeros(shape, jnp.int32), jnp.zeros(shape, jnp.int32)
        first = jnp.zeros((1, 1), jnp.int32)
        for trial in range(TRIALS):
            count = jnp.sum((trial_ref[...] <= trial).astype(jnp.int32), keepdims=True)
            low = jnp.where(label == trial, first, low)
            high = jnp.where(label == trial, count, high)
            first = count
        return low, high

    lane_low, lane_high = bounds((1, FLAT), 1)
    side_low, side_high = bounds((FLAT, 1), 0)
    spread = (
        lax.broadcasted_iota(jnp.int32, (RANK, FLAT), 1) % RANK
        == lax.broadcasted_iota(jnp.int32, (RANK, FLAT), 0)
    ).astype(jnp.bfloat16)

    def pick_rank(full, start):
        rows = full.shape[1]
        where = start + lax.broadcasted_iota(jnp.int32, (FLAT, rows), 1)
        mine = jnp.where((where >= side_low) & (where < side_high), full, 0.0)
        return jnp.sum(mine.reshape(TRIALS, RANK, rows), axis=0)

    def widen(low, start):
        values = lax.dot_general(low, spread, contract_first, preferred_element_type=jnp.float32)
        where = start + lax.broadcasted_iota(jnp.int32, values.shape, 0)
        return jnp.where((where >= lane_low) & (where < lane_high), values, 0.0).astype(jnp.bfloat16)

    down_load.wait()

    def cast_down(trial, carry):
        down_low[pl.ds(pl.multiple_of(trial * RANK, RANK), RANK), :] = down_v[trial].astype(jnp.bfloat16)
        return carry

    lax.fori_loop(0, TRIALS, cast_down, 0)
    own_rows = xg[pl.ds(pl.multiple_of(col * SHARD, SHARD), SHARD), :]
    hid_part[...] = pick_rank(
        lax.dot_general(down_low[...], own_rows, contract_last, preferred_element_type=jnp.float32), col * SHARD
    )
    go("hid_core")

    down_sum[...] = jnp.zeros_like(down_sum)
    total[...] = jnp.zeros_like(total)
    weight_load.wait()

    def hid_0():
        come("hid_core")
        hid_half[...] = hid_part[...] + hid_core[...]
        go("hid_far")

    def hid_1():
        come("hid_far")

        @pl.when(x == row)
        def _():
            hid_low[own_slot] = ((hid_half[...] + hid_far[...]) * INV_WIDTH).astype(jnp.bfloat16)
            go(*trio("hid_x"))

    def hid_2():
        for way in (1, 2, 3):
            @pl.when((x - way + 4) % 4 == row)
            def _():
                sends[f"hid_x{way}"]().wait_recv()

        go("hid_z")

    def hid_3():
        come("hid_z")
        go(*trio("hid_y"))

    def hid_4():
        come(*trio("hid_y"))

    def grad_0():
        up_load.wait()
        for trial in range(TRIALS):
            up_low[trial * RANK:(trial + 1) * RANK, :] = up_v[trial].astype(jnp.bfloat16)
        grad_load.wait()

        def gradient_chunk(chunk, carry):
            start = pl.multiple_of(chunk * 256, 256)
            full = lax.dot_general(
                up_low[...], grad_v[pl.ds(start, 256), :], contract_last, preferred_element_type=jnp.float32
            )
            grad_part[chunk] = pick_rank(full, row * 8 * SHARD + start)
            return carry

        lax.fori_loop(0, 4, gradient_chunk, 0)

    def grad_1():
        come("grad_z")
        grad_sum[...] = grad_part[...] + grad_z[...]
        go(*trio("grad_x"))
        grad_x[x] = grad_sum[x]

    def grad_2():
        come(*trio("grad_x"))
        grad_y[y] = (grad_x[0] + grad_x[1]) + (grad_x[2] + grad_x[3])
        go(*trio("grad_y"))

    def grad_3():
        come(*trio("grad_y"))
        gradient = (grad_y[0] + grad_y[1]) + (grad_y[2] + grad_y[3])
        grad_low[row * 4 + x] = (gradient * SCALE).astype(jnp.bfloat16)
        go(*trio("low_x"))

    def grad_4():
        come(*trio("low_x"))
        go("low_core")

    def grad_5():
        come("low_core")
        go("low_far")

    def widen_gradient(side):
        def wide(number, carry):
            chunk = side * 8 + number
            start = pl.multiple_of(chunk * 256, 256)
            grad_wide[pl.ds(start, 256), :] = widen(grad_low[chunk], start)
            return carry

        lax.fori_loop(0, 8, wide, 0)

    def grad_6():
        widen_gradient(z_hi)

    def grad_7():
        come("low_far")
        widen_gradient(1 - z_hi)

    def up_0():
        def wide(block, carry):
            start = pl.multiple_of(block * SHARD, SHARD)
            hid_wide[pl.ds(start, SHARD), :] = widen(hid_low[block], row * 8 * SHARD + start)
            return carry

        lax.fori_loop(0, 8, wide, 0)
        full = lax.dot_general(hid_wide[...], grad_v[...], contract_first, preferred_element_type=jnp.float32)
        up_part[...] = full.reshape(up_part.shape)
        go("up_core")

    def up_1():
        come("up_core")
        up_half[...] = (up_part[half] + up_core[...]).astype(jnp.bfloat16)
        go("up_far")

    def up_2():
        come("up_far")
        up_sum[half] = up_half[...].astype(jnp.float32) + up_far[...].astype(jnp.float32)
        go("up_share")

    def up_3():
        come("up_share")

        def moved(slot, carry):
            trial = keeper_ref[slot]
            new_up_ref[slot] = up_v[trial] - rate_ref[trial] * (up_sum[trial] * SCALE)
            return carry

        lax.fori_loop(0, TRIALS, moved, 0)

    def adapter_term():
        def adapter(block, carry):
            spot = pl.ds(pl.multiple_of(block * SHARD, SHARD), SHARD)
            total[spot, :] += SCALE * jnp.dot(
                hid_wide[spot, :], up_low[...], preferred_element_type=jnp.float32
            )
            return carry

        lax.fori_loop(0, 8, adapter, 0)

    ahead = {0: [hid_0], 2: [hid_1, grad_1], 4: [hid_2, grad_2], 6: [hid_3, grad_3], 8: [hid_4, grad_4],
             9: [grad_5], 10: [up_1], 12: [up_2]}
    after = {7: [], 8: [up_0], 9: [grad_6, adapter_term], 10: [grad_7], 13: [up_3]}
    grad_0()
    go("grad_z")

    def decode(code):
        dx, dy, dz, kind = code % 4, code // 4 % 4, code // 16 % 2, code // 32
        return (x + dx) % 4, base((dx, dy, dz, kind))

    def core_copy(slot):
        return pltpu.make_async_remote_copy(
            src_ref=stage.at[slot], dst_ref=recv_core.at[slot],
            send_sem=core_send.at[slot], recv_sem=core_recv.at[slot],
            device_id=core_mate, device_id_type=MESH,
        )

    def far_copy(number):
        spot = pl.ds(pl.multiple_of(number * PIECE, PIECE), PIECE)
        return pltpu.make_async_remote_copy(
            src_ref=z_stage.at[spot], dst_ref=recv_z.at[spot],
            send_sem=far_send.at[number], recv_sem=far_recv.at[number],
            device_id=far_mate, device_id_type=MESH,
        )

    def group_places(group):
        return [decode(select(group, [codes[slot] for codes in CODES])) for slot in range(4)]

    def group_rows(places):
        starts = [pl.multiple_of(start, PIECE) for _, start in places]
        return starts, jnp.concatenate([xg[pl.ds(start, PIECE), :] for start in starts], axis=0)

    def add_down(starts, rows):
        wide = jnp.concatenate([grad_wide[pl.ds(start, PIECE), :] for start in starts], axis=0)
        down_sum[...] += lax.dot_general(
            wide, rows, contract_first, preferred_element_type=jnp.float32
        ).reshape(down_sum.shape)

    def finish(group):
        places = group_places(group)
        for slot in range(4):
            plane, start = places[slot]

            @pl.when(plane == row)
            def _():
                number = start % (8 * SHARD) // PIECE
                far_copy(number).wait_recv()
                spot = pl.ds(pl.multiple_of(number * PIECE, PIECE), PIECE)
                proj_ref[spot, :] = (total[spot, :] + recv_z[spot, :].astype(jnp.float32)).astype(jnp.bfloat16)

    def add_core(place, own_sum, slot):
        plane, start = place
        number = start % (8 * SHARD) // PIECE
        spot = pl.ds(pl.multiple_of(number * PIECE, PIECE), PIECE)
        summed = own_sum + recv_core[slot].astype(jnp.float32)

        @pl.when(plane // 2 == z_hi)
        def _():
            total[spot, :] += summed

        @pl.when(plane // 2 != z_hi)
        def _():
            z_stage[spot, :] = summed.astype(jnp.bfloat16)
            far_copy(number).start()

    def hand_over(places, slots, product):
        for at, (plane, _) in enumerate(places):
            @pl.when(plane % 2 != core)
            def _():
                stage[slots[at]] = product[at * PIECE:(at + 1) * PIECE].astype(jnp.bfloat16)
                core_copy(slots[at]).start()

    def take_over(places, slots, own_sums):
        for at, place in enumerate(places):
            @pl.when(place[0] % 2 == core)
            def _():
                core_copy(slots[at]).wait_recv()
                add_core(place, own_sums[at * PIECE:(at + 1) * PIECE, :], slots[at])

    extra_places = group_places(GROUPS)

    def extra_product(part):
        places, slots = extra_places[2 * part:2 * part + 2], SLOTS[GROUPS][2 * part:2 * part + 2]
        _, rows = group_rows(places)
        product = jnp.dot(rows, w_v[...], preferred_element_type=jnp.float32)
        keep_half[...] = product
        hand_over(places, slots, product)

    def extra_sum(part):
        take_over(extra_places[2 * part:2 * part + 2], SLOTS[GROUPS][2 * part:2 * part + 2], keep_half)

    after[7].append(lambda: extra_product(0))
    after[8].insert(0, lambda: extra_sum(0))

    def body(group, carry):
        @pl.when(group == Z_GROUP)
        def _():
            for work in ahead.get(Z_GROUP, ()):
                work()

        for step in range(COUNT - 1):
            @pl.when(group == TURN[step])
            def _():
                arrive(step)
                if step == Z_GROUP - 1:
                    for kind in (0, 1):
                        z_copy(kind, 1).wait_recv()
                if step == SWAP_USED:
                    for kind in (0, 1):
                        swap(kind, 1).wait_recv()
                if step + 2 < COUNT:
                    send(step + 2)
                for work in ahead.get(TURN[step], ()):
                    work()
                if step >= 2:
                    sent(step - 2)
                if step == SWAP_SENT:
                    for kind in (0, 1):
                        swap(kind, 0).start()

        places = group_places(group)
        starts, rows = group_rows(places)
        product = jnp.dot(rows, w_v[...], preferred_element_type=jnp.float32)
        keep[...] = product
        slots = [select(group, [each[at] for each in SLOTS]) for at in range(4)]
        hand_over(places, slots, product)

        for at, works in after.items():
            @pl.when(group == at)
            def _():
                for work in works:
                    work()

        @pl.when(group >= CATCH_UP)
        def _():
            add_down(*group_rows(group_places(group)))

        take_over(places, slots, keep)

        @pl.when(group >= CATCH_UP)
        def _():
            def earlier(number, carry):
                before = (group - CATCH_UP - 1) * CATCH_EACH + 1 + number

                @pl.when((before >= 0) & (before < CATCH_UP))
                def _():
                    add_down(*group_rows(group_places(before)))

                return carry

            lax.fori_loop(0, CATCH_EACH, earlier, 0)

        @pl.when((group >= FINISH) & (group < FINISH + FINISHED // FINISH_EACH))
        def _():
            for number in range(FINISH_EACH):
                finish((group - FINISH) * FINISH_EACH + number)

        return carry

    lax.fori_loop(0, GROUPS, body, 0)

    def moved_down(slot, carry):
        trial = keeper_ref[slot]
        new_down_ref[slot] = down_v[trial] - rate_ref[trial] * (down_sum[trial] * INV_WIDTH)
        return carry

    arrive(COUNT - 1)
    extra_product(1)
    add_down(*group_rows(extra_places))
    lax.fori_loop(0, TRIALS, moved_down, 0)
    extra_sum(1)


    def last(group, carry):
        finish(group)
        return carry

    lax.fori_loop(FINISHED, GROUPS, last, 0)

    for step in range(COUNT - 3, COUNT):
        sent(step)
    for kind in (0, 1):
        swap(kind, 0).wait_send()
    for kind in (0, 1):
        z_copy(kind, 0).wait_send()
    for name in SMALL:
        if not name.startswith("hid_x"):
            sends[name]().wait_send()

    @pl.when(x == row)
    def _():
        for name in trio("hid_x"):
            sends[name]().wait_send()

    def drain(number, carry):
        core_copy(number).wait_send()
        return carry

    lax.fori_loop(0, SENT, drain, 0)
    finish(GROUPS)

    def drain_far(number, carry):
        far_copy(number).wait_send()
        return carry

    lax.fori_loop(0, 16, drain_far, 0)


def write_out(*refs):
    sources, targets, sems = refs[:3], refs[3:6], refs[6]
    copies = [pltpu.make_async_copy(sources[at], targets[at], sems.at[at]) for at in range(3)]
    for copy in copies:
        copy.start()
    for copy in copies:
        copy.wait()


def per_device(
    packed_input_rows,
    frozen_weight,
    down_adapters,
    up_adapters,
    trial_learning_rates,
    row_trial_index,
    output_gradient,
    keeper_slot,
):
    width_in, width_out = frozen_weight.shape
    all_rows = row_trial_index.shape[0]
    block_rows = output_gradient.shape[0]
    vmem = pl.BlockSpec(memory_space=pltpu.VMEM)
    smem = pl.BlockSpec(memory_space=pltpu.SMEM)
    hbm = pl.BlockSpec(memory_space=pl.ANY)
    dma = pltpu.SemaphoreType.DMA
    f32, bf16 = jnp.float32, jnp.bfloat16
    half = TRIALS // 2
    held = pl.pallas_call(
        whole_kernel,
        name="adapter_sweep",
        out_shape=(
            pltpu.VMEM((block_rows, width_out), bf16),
            pltpu.VMEM(down_adapters.shape, f32),
            pltpu.VMEM(up_adapters.shape, f32),
        ),
        in_specs=[hbm, hbm, hbm, hbm, smem, vmem, hbm, smem],
        out_specs=(vmem, vmem, vmem),
        scratch_shapes=[
            pltpu.VMEM((all_rows, width_in), bf16),
            pltpu.VMEM((width_in, width_out), bf16),
            pltpu.VMEM((4 * PIECE, width_out), f32),
            pltpu.VMEM((2 * PIECE, width_out), f32),
            pltpu.VMEM((SENT, PIECE, width_out), bf16),
            pltpu.VMEM((SENT, PIECE, width_out), bf16),
            pltpu.VMEM((block_rows, width_out), f32),
            pltpu.VMEM((block_rows, width_out), bf16),
            pltpu.VMEM((block_rows, width_out), bf16),
            pltpu.VMEM(down_adapters.shape, f32),
            pltpu.VMEM((FLAT, width_in), bf16),
            pltpu.VMEM(up_adapters.shape, f32),
            pltpu.VMEM((FLAT, width_out), bf16),
            pltpu.VMEM((block_rows, width_out), bf16),
            pltpu.VMEM(down_adapters.shape, f32),
            pltpu.VMEM((all_rows, FLAT), bf16),
            pltpu.VMEM((block_rows, FLAT), bf16),
            pltpu.VMEM((RANK, SHARD), f32),
            pltpu.VMEM((RANK, SHARD), f32),
            pltpu.VMEM((RANK, SHARD), f32),
            pltpu.VMEM((RANK, SHARD), f32),
            pltpu.VMEM((8, RANK, SHARD), bf16),
            pltpu.VMEM((4, RANK, 256), f32),
            pltpu.VMEM((4, RANK, 256), f32),
            pltpu.VMEM((4, RANK, 256), f32),
            pltpu.VMEM((4, RANK, 256), f32),
            pltpu.VMEM((4, RANK, 256), f32),
            pltpu.VMEM((16, RANK, 256), bf16),
            pltpu.VMEM((TRIALS, RANK, width_out), f32),
            pltpu.VMEM((half, RANK, width_out), f32),
            pltpu.VMEM((half, RANK, width_out), bf16),
            pltpu.VMEM((half, RANK, width_out), bf16),
            pltpu.VMEM((TRIALS, RANK, width_out), f32),
            dma((5,)),
            dma((2, 2, len(ITEMS))),
            dma((2, 2, len(ITEMS))),
            dma((2,)),
            dma((2,)),
            dma((2,)),
            dma((2,)),
            dma((SENT,)),
            dma((SENT,)),
            dma((16,)),
            dma((16,)),
            dma((len(SMALL),)),
            dma((len(SMALL),)),
        ],
        compiler_params=pltpu.CompilerParams(
            collective_id=0, has_side_effects=True, vmem_limit_bytes=56 << 20
        ),
        cost_estimate=pl.CostEstimate(flops=22 * 10**9, bytes_accessed=20 << 20, transcendentals=0),
    )(
        packed_input_rows, frozen_weight, down_adapters, up_adapters, trial_learning_rates,
        row_trial_index.reshape(32, all_rows // 32), output_gradient, keeper_slot,
    )
    held = [pltpu.with_memory_space_constraint(array, pltpu.VMEM) for array in held]
    return tuple(pl.pallas_call(
        write_out,
        name="write_out",
        out_shape=tuple(jax.ShapeDtypeStruct(array.shape, array.dtype) for array in held),
        in_specs=[vmem] * len(held),
        out_specs=tuple([hbm] * len(held)),
        scratch_shapes=[dma((len(held),))],
        compiler_params=pltpu.CompilerParams(vmem_limit_bytes=1 << 20),
    )(*held))


def solution(mesh):
    in_specs = (
        P("col", "row"),
        P("row", "col"),
        P(None, None, "row"),
        P(None, None, "col"),
        P(),
        P(),
        P("row", "col"),
        P(),
    )
    out_specs = (P("row", "col"), P(None, None, "row"), P(None, None, "col"))
    return jax.shard_map(
        per_device, mesh=mesh, in_specs=in_specs, out_specs=out_specs, check_vma=False
    )
```
